256 devices in a mesh: seq: 64 (over z, y, core), dp: 4 (over x).
Axes of the slice: x: 4, y: 4, z: 8, core: 2. Of those that a mesh axis runs over, the one named last changes fastest.
Arguments:
- queries: bfloat16 [4, 32768, 1024], P('dp', 'seq'), may hold values from -8 to 8
- memory_keys: bfloat16 [4, 32768, 1024], P('dp', 'seq'), may hold values from -8 to 8
- memory_values: bfloat16 [4, 32768, 1024], P('dp', 'seq'), may hold values from -6 to 6
- out_weight: bfloat16 [1024, 2048], P('seq'), may hold values from -0.1875 to 0.1875
- grad_out: bfloat16 [4, 32768, 2048], P('dp', 'seq'), may hold values from -6 to 6
- key_first: int32 [4, 256], P('dp', 'seq'), may hold values from 0 to 254, as said below
- key_last: int32 [4, 256], P('dp', 'seq'), may hold values from 2 to 256
Outputs:
- layer_out: bfloat16 [4, 32768, 2048], P('dp', 'seq')
- grad_query: bfloat16 [4, 32768, 1024], P('dp', 'seq')
- grad_keys: bfloat16 [4, 32768, 1024], P('dp', 'seq')
- grad_values: bfloat16 [4, 32768, 1024], P('dp', 'seq')
- weight_grad: float32 [1024, 2048], P('seq')
The draws below stay inside these ranges and needn't reach their ends.
Inputs may be any that keep to these rules, and one draw needn't show every extreme that they name: With key_last: query block b of pack p attends to key blocks key_first[p, b] to key_last[p, b] - 1, blocks of 128 tokens. Sentence pairs tile aligned groups of 4 blocks that begin at block 2, the first and last groups holding 4 // 2 blocks; a query block's key blocks lie in its own group and number 1 to 3, 3 in some group of every pack.
All inputs are finite; a program needn't handle non-finite values.
Results may differ from the reference program's by a relative error of at most 0.0095.
Values may be sent and summed in bfloat16 or wider, within the bound.
A program may use at most 192 MiB of HBM per device.

```python
import math
import jax
import jax.numpy as jnp
from jax import lax

D = 2048
HDIM = 128
HEADS = 8
BLOCK = 128
GROUP = 4
HD = 1024
SPAN = 3
TOKENS = 32768
QBLOCKS = 256
PACKS = 4


def pair_layout(key):
    inner_groups = QBLOCKS // GROUP - 1
    half_group = GROUP // 2
    split_query = jax.random.randint(jax.random.fold_in(key, 3), (PACKS, inner_groups), 1, GROUP)
    split_key = jax.random.randint(jax.random.fold_in(key, 4), (PACKS, inner_groups), 1, GROUP)
    split_key = split_key.at[:, 0].set(GROUP - 1)
    blocks = jnp.arange(QBLOCKS, dtype=jnp.int32)
    group_index = jnp.clip((blocks - half_group) // GROUP, 0, inner_groups - 1)
    within = blocks - half_group - group_index * GROUP
    group_start = half_group + group_index * GROUP
    query_split = split_query[:, group_index]
    key_split = split_key[:, group_index]
    early = within[None, :] < query_split
    first_block = jnp.where(early, group_start[None, :], group_start[None, :] + key_split)
    last_block = jnp.where(early, group_start[None, :] + key_split, group_start[None, :] + GROUP)
    leading = (blocks < half_group)[None, :]
    trailing = (blocks >= QBLOCKS - half_group)[None, :]
    first_block = jnp.where(leading, 0, jnp.where(trailing, QBLOCKS - half_group, first_block))
    last_block = jnp.where(leading, half_group, jnp.where(trailing, QBLOCKS, last_block))
    return (first_block.astype(jnp.int32), last_block.astype(jnp.int32))


def draw_key_first(key, part):
    return pair_layout(jax.random.fold_in(key, 1))[0]


def draw_key_last(key, part):
    return pair_layout(jax.random.fold_in(key, 1))[1]


def draw_queries(key, part):
    sample = jax.random.truncated_normal(jax.random.fold_in(key, 21), -4.0, 4.0, (PACKS, TOKENS, HD), jnp.float32)
    return sample.astype(jnp.bfloat16)


def draw_memory_keys(key, part):
    sample = jax.random.truncated_normal(jax.random.fold_in(key, 22), -4.0, 4.0, (PACKS, TOKENS, HD), jnp.float32)
    return sample.astype(jnp.bfloat16)


def level_of(rng, shape, pieces, low, top_value):
    gain, own = 1.0, jax.random.fold_in(rng, 6)
    for dim, parts in pieces:
        heights = jnp.exp(jax.random.uniform(jax.random.fold_in(own, dim), (parts,), jnp.float32, low / len(pieces), top_value / len(pieces)))
        gain = gain * jnp.repeat(heights, shape[dim] // parts).reshape([-1 if axis == dim else 1 for axis in range(len(shape))])
    return gain


def noise(key, extent, deviation, bound, split=(), kind=jnp.bfloat16):
    values = deviation * jax.random.normal(key, extent, jnp.float32)
    if split:
        values = values * level_of(key, extent, split, -0.22, 0.18)
    return jnp.clip(values, -bound, bound).astype(kind)


def setup_inputs(seed: int = 0) -> dict:
    streams_of = jax.random.split(jax.random.key(seed), 8)
    return {
        "queries": draw_queries(jax.random.fold_in(streams_of[7], 71), 0),
        "memory_keys": draw_memory_keys(jax.random.fold_in(streams_of[7], 71), 0),
        "memory_values": noise(streams_of[2], (PACKS, TOKENS, HD), 1.0, 6.0, ((0, 4), (1, 64))),
        "out_weight": noise(streams_of[3], (HD, D), HD ** -0.5, 0.1875, ((0, 64),)),
        "grad_out": noise(streams_of[4], (PACKS, TOKENS, D), 1.0, 6.0, ((0, 4), (1, 64))),
        "key_first": draw_key_first(jax.random.fold_in(streams_of[7], 71), 0),
        "key_last": draw_key_last(jax.random.fold_in(streams_of[7], 71), 0),
    }


def attend_block(query_rows, key_rows, value_rows, grad_rows, allowed):
    score_scale = 1.0 / math.sqrt(HDIM)
    query_heads = query_rows.reshape(BLOCK, HEADS, HDIM).astype(jnp.float32)
    key_heads = key_rows.reshape(-1, HEADS, HDIM).astype(jnp.float32)
    value_heads = value_rows.reshape(-1, HEADS, HDIM).astype(jnp.float32)
    grad_heads = grad_rows.reshape(BLOCK, HEADS, HDIM).astype(jnp.float32)
    scores = jnp.einsum('qhd,khd->hqk', query_heads, key_heads) * score_scale
    inside = allowed[None, None, :]
    highest = lax.optimization_barrier(jnp.max(jnp.where(inside, scores, -jnp.inf), axis=-1, keepdims=True))
    raised = jnp.where(inside, jnp.exp(scores - highest), 0.0)
    softmax_probs = raised / lax.optimization_barrier(jnp.sum(raised, axis=-1, keepdims=True))
    weights = lax.optimization_barrier(softmax_probs.astype(jnp.bfloat16)).astype(jnp.float32)
    attended = jnp.einsum('hqk,khd->qhd', weights, value_heads).astype(jnp.bfloat16)
    grad_probs = jnp.einsum('qhd,khd->hqk', grad_heads, value_heads)
    row_term = lax.optimization_barrier(jnp.sum(softmax_probs * grad_probs, axis=-1, keepdims=True))
    grad_scores = (softmax_probs * (grad_probs - row_term) * score_scale).astype(jnp.bfloat16)
    grad_scores = lax.optimization_barrier(grad_scores).astype(jnp.float32)
    grad_query = jnp.einsum('hqk,khd->qhd', grad_scores, key_heads).astype(jnp.bfloat16)
    key_part = jnp.einsum('hqk,qhd->khd', grad_scores, query_heads)
    value_part = jnp.einsum('hqk,qhd->khd', weights, grad_heads)
    return (attended.reshape(BLOCK, HD), grad_query.reshape(BLOCK, HD), key_part.reshape(-1, HD), value_part.reshape(-1, HD))

def one_pack(packed):
    pack_queries, pack_keys, pack_values, pack_grads, pack_first, pack_last = packed
    window_rows = SPAN * BLOCK

    def advance(running, block_index):
        key_acc, value_acc = running
        first_block = pack_first[block_index]
        last_block = pack_last[block_index]
        anchor = jnp.minimum(first_block * BLOCK, TOKENS - window_rows).astype(jnp.int32)
        row_start = (block_index * BLOCK).astype(jnp.int32)
        query_rows = lax.dynamic_slice_in_dim(pack_queries, row_start, BLOCK, 0)
        grad_rows = lax.dynamic_slice_in_dim(pack_grads, row_start, BLOCK, 0)
        key_rows = lax.dynamic_slice_in_dim(pack_keys, anchor, window_rows, 0)
        value_rows = lax.dynamic_slice_in_dim(pack_values, anchor, window_rows, 0)
        block_ids = (anchor + jnp.arange(window_rows, dtype=jnp.int32)) // BLOCK
        allowed = (block_ids >= first_block) & (block_ids < last_block)
        attended, grad_query, key_part, value_part = attend_block(query_rows, key_rows, value_rows, grad_rows, allowed)
        key_acc = lax.dynamic_update_slice_in_dim(key_acc, lax.dynamic_slice_in_dim(key_acc, anchor, window_rows, 0) + key_part, anchor, 0)
        value_acc = lax.dynamic_update_slice_in_dim(value_acc, lax.dynamic_slice_in_dim(value_acc, anchor, window_rows, 0) + value_part, anchor, 0)
        return ((key_acc, value_acc), (attended, grad_query))
    empty_sum = jnp.zeros((TOKENS, HD), jnp.float32)
    sums, outputs = lax.scan(advance, (empty_sum, empty_sum), jnp.arange(QBLOCKS, dtype=jnp.int32))
    attended = outputs[0].reshape(TOKENS, HD)
    grad_query = outputs[1].reshape(TOKENS, HD)
    return (attended, grad_query, sums[0].astype(jnp.bfloat16), sums[1].astype(jnp.bfloat16))

def reference(queries, memory_keys, memory_values, out_weight, grad_out, key_first, key_last):
    flat_grad = grad_out.reshape(PACKS * TOKENS, D)
    grad_attn = lax.dot_general(flat_grad, out_weight, (((1,), (1,)), ((), ())), preferred_element_type=jnp.float32).astype(jnp.bfloat16)
    grad_attn = grad_attn.reshape(PACKS, TOKENS, HD)
    attended, grad_query, grad_keys, grad_values = lax.map(one_pack, (queries, memory_keys, memory_values, grad_attn, key_first, key_last))
    flat_attn = attended.reshape(PACKS * TOKENS, HD)
    layer_out = jnp.dot(flat_attn, out_weight, preferred_element_type=jnp.float32).astype(jnp.bfloat16)
    layer_out = layer_out.reshape(PACKS, TOKENS, D)
    weight_grad = lax.dot_general(flat_attn, flat_grad, (((0,), (0,)), ((), ())), preferred_element_type=jnp.float32) / math.sqrt(TOKENS)
    return (layer_out, grad_query, grad_keys, grad_values, weight_grad)
```

```python
import functools
import math

import jax
import jax.numpy as jnp
from jax import lax
from jax.experimental import pallas as pl
from jax.experimental.pallas import tpu as pltpu
from jax.sharding import PartitionSpec as P

HDIM = 128
BLOCK = 128
HALF = 256
CORES = 2
Y_CHIPS = 4
F32 = jnp.float32
BF16 = jnp.bfloat16
NEVER = -1e30


def dot(a, b, dims):
    return lax.dot_general(a, b, (dims, ((), ())), preferred_element_type=F32)


def kernel(
    sizes,
    q_hbm, k_hbm, v_hbm, shard_hbm, go_hbm, first_ref, last_ref,
    layer_hbm, dq_hbm, dk_hbm, dv_hbm, wgrad_hbm,
    w, q, kg, vg, go, probs, attn_t, attn, ga, bias,
    dq, dk_own, dv_own, dk_send, dv_send, dk_recv, dv_recv, layer,
    wg, sib_recv, plus_send, plus_recv, minus_send, minus_recv,
    z_sum, y_send, y_recv, x_all, wgrad,
    load_sem, store_sem,
    halo_send_sem, halo_recv_sem,
    agy_send_sem, agy_recv_sem, agp_send_sem, agp_recv_sem, agm_send_sem, agm_recv_sem,
    ags_send_sem, ags_recv_sem,
    rss_send_sem, rss_recv_sem, rsp_send_sem, rsp_recv_sem, rsm_send_sem, rsm_recv_sem,
    rsy_send_sem, rsy_recv_sem, rsx_send_sem, rsx_recv_sem,
    grad_send_sem, grad_recv_sem,
):
    n_seq, n_x, n_y, n_z, n_plus, n_minus, heads, width, norm = sizes
    scale = 1.0 / math.sqrt(HDIM)
    s = lax.axis_index("seq")
    x = lax.axis_index("dp")
    c = s % CORES
    zy = s // CORES
    y = zy % n_y
    z = zy // n_y

    def at_zy(z_index, y_index, core):
        return (z_index * n_y + y_index) * CORES + core

    sibling = s + 1 - 2 * c
    across = (s + 2 * c - 1 + n_seq) % n_seq
    z_next = at_zy((z + 1) % n_z, y, c)
    z_prev = at_zy((z + n_z - 1) % n_z, y, c)
    y_peers = [at_zy(z, (y + j) % n_y, c) for j in range(1, n_y)]
    x_peers = [(x + j) % n_x for j in range(1, n_x)]
    partners = (sibling, across)
    group = (1 - c, c)

    loads = []

    def load(src, dst):
        copy = pltpu.make_async_copy(src, dst, load_sem.at[len(loads)])
        copy.start()
        loads.append(copy)
        return copy

    def token_rows(t):
        return pl.ds(pl.multiple_of(group[t] * HALF, HALF), HALF)

    load_shard = load(shard_hbm, w.at[zy, c])
    load_q, load_k, load_v, load_go = [], [], [], []
    for t in range(2):
        load_q.append(load(q_hbm.at[token_rows(t)], q.at[t]))
        load_k.append(load(k_hbm.at[token_rows(t)], kg.at[t, pl.ds(0, HALF)]))
        load_v.append(load(v_hbm.at[token_rows(t)], vg.at[t, pl.ds(0, HALF)]))
    for t in range(2):
        load_go.append(load(go_hbm.at[token_rows(t)], go.at[t]))

    barrier = pltpu.get_barrier_semaphore()
    seq_peers = [sibling, across, z_next, z_prev] + y_peers
    for peer in seq_peers:
        pl.semaphore_signal(
            barrier, inc=1, device_id={"seq": peer}, device_id_type=pl.DeviceIdType.MESH
        )
    for peer in x_peers:
        pl.semaphore_signal(
            barrier, inc=1, device_id={"dp": peer}, device_id_type=pl.DeviceIdType.MESH
        )
    pl.semaphore_wait(barrier, len(seq_peers) + len(x_peers))

    sent = []

    def send(src, dst, send_sem, recv_sem, target):
        copy = pltpu.make_async_remote_copy(
            src_ref=src,
            dst_ref=dst,
            send_sem=send_sem,
            recv_sem=recv_sem,
            device_id=target,
            device_id_type=pl.DeviceIdType.MESH,
        )
        copy.start()
        sent.append(copy)
        return copy

    agy = [
        send(
            shard_hbm, w.at[zy, c], agy_send_sem.at[j], agy_recv_sem.at[j], {"seq": peer}
        )
        for j, peer in enumerate(y_peers)
    ]

    halo = []
    for t in (1, 0):
        for which, (src, dst) in enumerate(((k_hbm, kg), (v_hbm, vg))):
            halo.append(
                send(
                    src.at[token_rows(t)],
                    dst.at[t, pl.ds(HALF, HALF)],
                    halo_send_sem.at[t * 2 + which],
                    halo_recv_sem.at[t * 2 + which],
                    {"seq": partners[t]},
                )
            )
    halo = {1: halo[:2], 0: halo[2:]}

    def slab(z_index):
        return w.at[pl.ds(z_index * n_y, n_y), c]

    ag_sib = []

    def share_slab(z_index):
        i = len(ag_sib)
        ag_sib.append(
            send(
                slab(z_index), slab(z_index), ags_send_sem.at[i], ags_recv_sem.at[i],
                {"seq": sibling},
            )
        )

    agp, agm = [], []

    def ag_step(k):
        if k == 0:
            load_shard.wait()
            for copy in agy:
                copy.wait_recv()
        from_prev, from_next = (z + n_z - k) % n_z, (z + k) % n_z
        if 0 < k <= n_plus:
            agp[k - 1].wait_recv()
        if k < n_plus:
            agp.append(
                send(
                    slab(from_prev), slab(from_prev), agp_send_sem.at[k], agp_recv_sem.at[k],
                    {"seq": z_next},
                )
            )
        if 0 < k <= n_minus:
            agm[k - 1].wait_recv()
        if k < n_minus:
            agm.append(
                send(
                    slab(from_next), slab(from_next), agm_send_sem.at[k], agm_recv_sem.at[k],
                    {"seq": z_prev},
                )
            )
        if k <= n_plus:
            share_slab(from_prev)
        if 0 < k <= n_minus:
            share_slab(from_next)

    for t in range(2):
        key_row = lax.broadcasted_iota(jnp.int32, (2 * HALF, HALF), 0)
        query_col = lax.broadcasted_iota(jnp.int32, (2 * HALF, HALF), 1)
        own_base = s * 4 + 2 * group[t]
        halo_base = s * 4 - 2 + 6 * group[t]
        key_block = jnp.where(
            key_row < HALF,
            own_base + (key_row >> 7),
            halo_base - 2 + (key_row >> 7),
        )
        early = query_col < BLOCK
        lower = jnp.where(early, first_ref[0, 2 * group[t]], first_ref[0, 2 * group[t] + 1])
        upper = jnp.where(early, last_ref[0, 2 * group[t]], last_ref[0, 2 * group[t] + 1])
        inside = (key_block >= lower) & (key_block < upper)
        bias[t] = jnp.where(inside, 0.0, NEVER)

    def columns(h):
        return pl.ds(pl.multiple_of(h * HDIM, HDIM), HDIM)

    def forward(t):
        load_q[t].wait()
        load_k[t].wait()
        load_v[t].wait()
        for copy in halo[t]:
            copy.wait_recv()

        def head(h, carry):
            cols = columns(h)
            scores = dot(kg[t, :, cols], q[t, :, cols], ((1,), (1,))) * scale + bias[t]
            highest = jnp.max(scores, axis=0, keepdims=True)
            raised = jnp.exp(scores - highest)
            total = jnp.sum(raised, axis=0, keepdims=True)
            p = raised * (1.0 / total)
            probs[t, h] = p
            out_t = dot(vg[t, :, cols], p.astype(BF16), ((0,), (0,)))
            attn_t[pl.ds(pl.multiple_of(h * HDIM, HDIM), HDIM), pl.ds(t * HALF, HALF)] = (
                out_t.astype(BF16)
            )
            attn[pl.ds(t * HALF, HALF), cols] = out_t.T.astype(BF16)
            return carry

        lax.fori_loop(0, heads, head, 0)

    def backward(t):
        def head(h, carry):
            cols = columns(h)
            p = probs[t, h]
            grad_rows = ga[pl.ds(t * HALF, HALF), cols]
            grad_p = dot(vg[t, :, cols], grad_rows, ((1,), (1,)))
            row_term = jnp.sum(p * grad_p, axis=0, keepdims=True)
            grad_s = (p * (grad_p - row_term) * scale).astype(BF16)
            dq_t = dot(kg[t, :, cols], grad_s, ((0,), (0,)))
            dq[t, :, cols] = dq_t.T.astype(BF16)
            dk = dot(grad_s, q[t, :, cols], ((1,), (0,)))
            dv = dot(p.astype(BF16), grad_rows, ((1,), (0,)))
            dk_own[t, :, cols] = dk[:HALF]
            dv_own[t, :, cols] = dv[:HALF]
            dk_send[t, :, cols] = dk[HALF:].astype(BF16)
            dv_send[t, :, cols] = dv[HALF:].astype(BF16)
            return carry

        lax.fori_loop(0, heads, head, 0)
        return [
            send(
                src.at[t], dst.at[t], grad_send_sem.at[2 * t + i], grad_recv_sem.at[2 * t + i],
                {"seq": partners[t]},
            )
            for i, (src, dst) in enumerate(((dk_send, dk_recv), (dv_send, dv_recv)))
        ]

    ag_step(0)
    forward(0)
    ag_step(1)
    forward(1)
    if n_plus >= 2:
        ag_step(2)

    for copy in load_go:
        copy.wait()
    hd = heads * HDIM
    row_blocks, col_width = hd // HALF, min(512, width)

    def weight_tile(i, carry):
        r, n = i % row_blocks, i // row_blocks
        cols = pl.ds(pl.multiple_of(n * col_width, col_width), col_width)
        left = attn_t[pl.ds(pl.multiple_of(r * HALF, HALF), HALF), :]
        right = go[:, :, cols].reshape(2 * HALF, col_width)
        tile = dot(left, right, ((1,), (0,))).astype(BF16)
        wg[pl.ds(r * 8, 8), :, :, cols] = tile.reshape(8, CORES, 16, col_width)
        return carry

    lax.fori_loop(0, row_blocks * (width // col_width), weight_tile, 0)

    order = []
    for k in range(max(n_plus, n_minus), 0, -1):
        if k <= n_plus:
            order.append((1, k))
        if k <= n_minus:
            order.append((-1, k))
    order.append((1, 0))
    rss = {}
    for i, (way, k) in enumerate(order):
        d = (z + way * k + n_z) % n_z
        rss[way, k] = send(
            wg.at[pl.ds(d * n_y, n_y), 1 - c], sib_recv.at[i], rss_send_sem.at[i],
            rss_recv_sem.at[i], {"seq": sibling},
        )
    rsp, rsm = {}, {}

    def chain(way, k):
        i = order.index((way, k))
        d = (z + way * k + n_z) % n_z
        rss[way, k].wait_recv()
        arrivals = []
        if (way == 1 or k == 0) and k < n_plus:
            rsp[k + 1].wait_recv()
            arrivals.append(plus_recv)
        if (way == -1 or k == 0) and k < n_minus:
            rsm[k + 1].wait_recv()
            arrivals.append(minus_recv)

        def add(j, carry):
            total = wg[d * n_y + j, c].astype(F32) + sib_recv[i, j].astype(F32)
            for ref in arrivals:
                total = total + ref[k, j].astype(F32)
            if k == 0:
                z_sum[j] = total
                y_send[j] = total.astype(BF16)
            elif way == 1:
                plus_send[k - 1, j] = total.astype(BF16)
            else:
                minus_send[k - 1, j] = total.astype(BF16)
            return carry

        lax.fori_loop(0, n_y, add, 0)
        if k and way == 1:
            rsp[k] = send(
                plus_send.at[k - 1], plus_recv.at[k - 1], rsp_send_sem.at[k - 1],
                rsp_recv_sem.at[k - 1], {"seq": z_next},
            )
        if k and way == -1:
            rsm[k] = send(
                minus_send.at[k - 1], minus_recv.at[k - 1], rsm_send_sem.at[k - 1],
                rsm_recv_sem.at[k - 1], {"seq": z_prev},
            )

    def chain_level(k):
        if k <= n_plus:
            chain(1, k)
        if 0 < k <= n_minus:
            chain(-1, k)

    chain_level(n_plus)
    for k in range(3, n_plus + 1):
        ag_step(k)
    for copy in ag_sib:
        copy.wait_recv()

    def grad_tile(i, carry):
        rows = w[pl.ds(i * 8, 8)].reshape(HALF, width)
        tile = dot(go[...].reshape(2 * HALF, width), rows, ((1,), (1,)))
        ga[:, pl.ds(pl.multiple_of(i * HALF, HALF), HALF)] = tile.astype(BF16)
        return carry

    lax.fori_loop(0, row_blocks, grad_tile, 0)

    levels = list(range(n_plus - 1, 0, -1))
    grads = {}
    if levels:
        chain_level(levels.pop(0))
    grads[1] = backward(1)
    if levels:
        chain_level(levels.pop(0))
    grads[0] = backward(0)
    for k in levels:
        chain_level(k)
    chain_level(0)

    stores = []

    def store(src, dst):
        copy = pltpu.make_async_copy(src, dst, store_sem.at[len(stores)])
        copy.start()
        stores.append(copy)

    rsy = [
        send(
            y_send.at[(y + j) % n_y], y_recv.at[j - 1], rsy_send_sem.at[j - 1],
            rsy_recv_sem.at[j - 1], {"seq": peer},
        )
        for j, peer in enumerate(y_peers, 1)
    ]
    for t in range(2):
        store(dq.at[t], dq_hbm.at[token_rows(t)])

    tiles = width // HALF

    def layer_tile(i, carry):
        cols = pl.ds(pl.multiple_of(i * HALF, HALF), HALF)
        right = w[:, :, :, cols].reshape(hd, HALF)
        layer[:, cols] = dot(attn[...], right, ((1,), (0,))).astype(BF16)
        return carry

    lax.fori_loop(0, tiles // 2, layer_tile, 0)

    total = z_sum[y]
    for j, copy in enumerate(rsy):
        copy.wait_recv()
        total = total + y_recv[j].astype(F32)
    x_all[x] = total.astype(BF16)
    rsx = [
        send(
            x_all.at[x], x_all.at[x], rsx_send_sem.at[j], rsx_recv_sem.at[j], {"dp": peer}
        )
        for j, peer in enumerate(x_peers)
    ]
    lax.fori_loop(tiles // 2, tiles, layer_tile, 0)
    for t in range(2):
        store(layer.at[pl.ds(t * HALF, HALF)], layer_hbm.at[token_rows(t)])

    for t in (0, 1):
        for copy in grads[t]:
            copy.wait()
        for own, got, out, hbm in (
            (dk_own, dk_recv, dk_send, dk_hbm), (dv_own, dv_recv, dv_send, dv_hbm)
        ):
            def add_rows(i, carry, own=own, got=got, out=out, t=t):
                rows = pl.ds(pl.multiple_of(i * 32, 32), 32)
                out[t, rows] = (own[t, rows] + got[t, rows].astype(F32)).astype(BF16)
                return carry

            lax.fori_loop(0, HALF // 32, add_rows, 0)
            store(out.at[t], hbm.at[token_rows(t)])

    for copy in rsx:
        copy.wait_recv()
    total = x_all[0].astype(F32)
    for j in range(1, n_x):
        total = total + x_all[j].astype(F32)
    wgrad[...] = total * (1.0 / norm)
    store(wgrad, wgrad_hbm)

    waited = grads[0] + grads[1]
    for copy in sent:
        if not any(copy is other for other in waited):
            copy.wait_send()
    for copy in stores:
        copy.wait()


def body(n_seq, n_x, n_y, queries, memory_keys, memory_values, out_weight, grad_out, key_first, key_last):
    rows, hd = queries.shape[1:]
    width = grad_out.shape[2]
    heads = hd // HDIM
    n_z = n_seq // (CORES * n_y)
    n_plus = n_z // 2
    n_minus = n_z - 1 - n_plus
    n_zy = n_z * n_y
    norm = math.sqrt(n_seq * rows)
    sizes = (n_seq, n_x, n_y, n_z, n_plus, n_minus, heads, width, norm)
    vmem, dma = pltpu.VMEM, pltpu.SemaphoreType.DMA
    scratch = [
        vmem((n_zy, CORES, 16, width), BF16),
        vmem((2, HALF, hd), BF16),
        vmem((2, 2 * HALF, hd), BF16),
        vmem((2, 2 * HALF, hd), BF16),
        vmem((2, HALF, width), BF16),
        vmem((2, heads, 2 * HALF, HALF), F32),
        vmem((hd, 2 * HALF), BF16),
        vmem((2 * HALF, hd), BF16),
        vmem((2 * HALF, hd), BF16),
        vmem((2, 2 * HALF, HALF), F32),
        vmem((2, HALF, hd), BF16),
        vmem((2, HALF, hd), F32),
        vmem((2, HALF, hd), F32),
        vmem((2, HALF, hd), BF16),
        vmem((2, HALF, hd), BF16),
        vmem((2, HALF, hd), BF16),
        vmem((2, HALF, hd), BF16),
        vmem((2 * HALF, width), BF16),
        vmem((n_zy, CORES, 16, width), BF16),
        vmem((n_z, n_y, 16, width), BF16),
        vmem((n_plus, n_y, 16, width), BF16),
        vmem((n_plus, n_y, 16, width), BF16),
        vmem((max(n_minus, 1), n_y, 16, width), BF16),
        vmem((max(n_minus, 1), n_y, 16, width), BF16),
        vmem((n_y, 16, width), F32),
        vmem((n_y, 16, width), BF16),
        vmem((n_y - 1, 16, width), BF16),
        vmem((n_x, 16, width), BF16),
        vmem((16, width), F32),
        dma((9,)),
        dma((9,)),
        dma((4,)), dma((4,)),
        dma((n_y - 1,)), dma((n_y - 1,)),
        dma((n_plus,)), dma((n_plus,)),
        dma((max(n_minus, 1),)), dma((max(n_minus, 1),)),
        dma((n_z,)), dma((n_z,)),
        dma((n_z,)), dma((n_z,)),
        dma((n_plus,)), dma((n_plus,)),
        dma((max(n_minus, 1),)), dma((max(n_minus, 1),)),
        dma((n_y - 1,)), dma((n_y - 1,)),
        dma((n_x - 1,)), dma((n_x - 1,)),
        dma((4,)), dma((4,)),
    ]
    hbm = pl.BlockSpec(memory_space=pl.ANY)
    smem = pl.BlockSpec(memory_space=pltpu.SMEM)
    layer_out, grad_query, grad_keys, grad_values, weight_grad = pl.pallas_call(
        functools.partial(kernel, sizes),
        out_shape=(
            jax.ShapeDtypeStruct((rows, width), BF16),
            jax.ShapeDtypeStruct((rows, hd), BF16),
            jax.ShapeDtypeStruct((rows, hd), BF16),
            jax.ShapeDtypeStruct((rows, hd), BF16),
            jax.ShapeDtypeStruct((16, width), F32),
        ),
        in_specs=[hbm] * 5 + [smem] * 2,
        out_specs=(hbm,) * 5,
        scratch_shapes=scratch,
        compiler_params=pltpu.CompilerParams(
            collective_id=0, has_side_effects=True, vmem_limit_bytes=60 * 1024 * 1024
        ),
    )(
        queries[0], memory_keys[0], memory_values[0], out_weight, grad_out[0], key_first, key_last
    )
    return (layer_out[None], grad_query[None], grad_keys[None], grad_values[None], weight_grad)


def solution(mesh, n_y=Y_CHIPS):
    return jax.shard_map(
        functools.partial(body, mesh.shape["seq"], mesh.shape["dp"], n_y),
        mesh=mesh,
        in_specs=(
            P("dp", "seq", None),
            P("dp", "seq", None),
            P("dp", "seq", None),
            P("seq", None),
            P("dp", "seq", None),
            P("dp", "seq"),
            P("dp", "seq"),
        ),
        out_specs=(
            P("dp", "seq", None),
            P("dp", "seq", None),
            P("dp", "seq", None),
            P("dp", "seq", None),
            P("seq", None),
        ),
        check_vma=False,
    )
```

```python
import functools
import math

import jax
import jax.numpy as jnp
from jax import lax
from jax.experimental import pallas as pl
from jax.experimental.pallas import tpu as pltpu
from jax.sharding import PartitionSpec as P

HDIM = 128
BLOCK = 128
HALF = 256
CORES = 2
Y_CHIPS = 4
F32 = jnp.float32
BF16 = jnp.bfloat16
NEVER = -1e30


def dot(a, b, dims):
    return lax.dot_general(a, b, (dims, ((), ())), preferred_element_type=F32)


def kernel(
    sizes,
    q_hbm, k_hbm, v_hbm, shard_hbm, go_hbm, first_ref, last_ref,
    layer_hbm, dq_hbm, dk_hbm, dv_hbm, wgrad_hbm,
    w, q, kg, vg, go, probs, attn_t, attn, ga, bias,
    dq, dk_own, dv_own, dk_send, dv_send, dk_recv, dv_recv, layer,
    wg, sib_recv, side_send, side_recv, plus_send, plus_recv, minus_send, minus_recv,
    z_sum, y_send, y_recv, x_all, wgrad,
    load_sem, store_sem,
    halo_send_sem, halo_recv_sem,
    agy_send_sem, agy_recv_sem, agp_send_sem, agp_recv_sem, agm_send_sem, agm_recv_sem,
    agx_send_sem, agx_recv_sem, ags_send_sem, ags_recv_sem,
    rsw_send_sem, rsw_recv_sem,
    rss_send_sem, rss_recv_sem, rsp_send_sem, rsp_recv_sem, rsm_send_sem, rsm_recv_sem,
    rsy_send_sem, rsy_recv_sem, rsx_send_sem, rsx_recv_sem,
    grad_send_sem, grad_recv_sem,
):
    n_seq, n_x, n_y, n_z, n_plus, n_minus, heads, width, norm = sizes
    scale = 1.0 / math.sqrt(HDIM)
    s = lax.axis_index("seq")
    x = lax.axis_index("dp")
    c = s % CORES
    zy = s // CORES
    y = zy % n_y
    z = zy // n_y

    def at_zy(z_index, y_index, core):
        return (z_index * n_y + y_index) * CORES + core

    sibling = s + 1 - 2 * c
    across = (s + 2 * c - 1 + n_seq) % n_seq
    z_next = at_zy((z + 1) % n_z, y, c)
    z_prev = at_zy((z + n_z - 1) % n_z, y, c)
    y_peers = [at_zy(z, (y + j) % n_y, c) for j in range(1, n_y)]
    x_peers = [(x + j) % n_x for j in range(1, n_x)]
    x_next, x_prev = (x + 1) % n_x, (x + n_x - 1) % n_x
    half, quarter = width // 2, width // 4
    mine, other = (x % 2) * half, (1 - x % 2) * half

    def wide(start, size):
        return pl.ds(pl.multiple_of(start, 128), size)

    partners = (sibling, across)
    group = (1 - c, c)

    loads = []

    def load(src, dst):
        copy = pltpu.make_async_copy(src, dst, load_sem.at[len(loads)])
        copy.start()
        loads.append(copy)
        return copy

    def token_rows(t):
        return pl.ds(pl.multiple_of(group[t] * HALF, HALF), HALF)

    load_shard = load(shard_hbm, w.at[zy, c])
    load_q, load_k, load_v, load_go = [], [], [], []
    for t in range(2):
        load_q.append(load(q_hbm.at[token_rows(t)], q.at[t]))
        load_k.append(load(k_hbm.at[token_rows(t)], kg.at[t, pl.ds(0, HALF)]))
        load_v.append(load(v_hbm.at[token_rows(t)], vg.at[t, pl.ds(0, HALF)]))
    for t in range(2):
        load_go.append(load(go_hbm.at[token_rows(t)], go.at[t]))

    barrier = pltpu.get_barrier_semaphore()
    seq_peers = [sibling, across, z_next, z_prev] + y_peers
    for peer in seq_peers:
        pl.semaphore_signal(
            barrier, inc=1, device_id={"seq": peer}, device_id_type=pl.DeviceIdType.MESH
        )
    for peer in x_peers:
        pl.semaphore_signal(
            barrier, inc=1, device_id={"dp": peer}, device_id_type=pl.DeviceIdType.MESH
        )
    pl.semaphore_wait(barrier, len(seq_peers) + len(x_peers))

    sent = []

    def send(src, dst, send_sem, recv_sem, target):
        copy = pltpu.make_async_remote_copy(
            src_ref=src,
            dst_ref=dst,
            send_sem=send_sem,
            recv_sem=recv_sem,
            device_id=target,
            device_id_type=pl.DeviceIdType.MESH,
        )
        copy.start()
        sent.append(copy)
        return copy

    agy = [
        send(
            shard_hbm, w.at[zy, c], agy_send_sem.at[j], agy_recv_sem.at[j], {"seq": peer}
        )
        for j, peer in enumerate(y_peers)
    ]

    hd = heads * HDIM
    head_parts = ((0, heads // 2), (heads // 2, heads))

    def part_cols(part):
        low, high = head_parts[part]
        return pl.ds(low * HDIM, (high - low) * HDIM)

    halo = {}
    for t in (1, 0):
        for part in range(2):
            halo[t, part] = []
            for which, (src, dst) in enumerate(((k_hbm, kg), (v_hbm, vg))):
                i = (t * 2 + part) * 2 + which
                halo[t, part].append(
                    send(
                        src.at[token_rows(t), part_cols(part)],
                        dst.at[t, pl.ds(HALF, HALF), part_cols(part)],
                        halo_send_sem.at[i],
                        halo_recv_sem.at[i],
                        {"seq": partners[t]},
                    )
                )

    def slab(z_index, start, size):
        return w.at[pl.ds(z_index * n_y, n_y), c, :, wide(start, size)]

    ag_sib, ag_side = [], {}

    def share_slab(z_index, start, size):
        i = len(ag_sib)
        piece = slab(z_index, start, size)
        ag_sib.append(
            send(piece, piece, ags_send_sem.at[i], ags_recv_sem.at[i], {"seq": sibling})
        )

    def pass_aside(z_index, key):
        ag_side[key] = []
        for start, peer in ((mine, x_next), (mine + quarter, x_prev)):
            i = 2 * len(ag_side) - 2 + len(ag_side[key])
            piece = slab(z_index, start, quarter)
            ag_side[key].append(
                send(piece, piece, agx_send_sem.at[i], agx_recv_sem.at[i], {"dp": peer})
            )

    agp, agm = [], []

    def ag_step(k):
        if k == 0:
            load_shard.wait()
            for copy in agy:
                copy.wait_recv()
        from_prev, from_next = (z + n_z - k) % n_z, (z + k) % n_z
        if 0 < k <= n_plus:
            agp[k - 1].wait_recv()
        if k < n_plus:
            piece = slab(from_prev, mine, half)
            agp.append(
                send(piece, piece, agp_send_sem.at[k], agp_recv_sem.at[k], {"seq": z_next})
            )
        if 0 < k <= n_plus:
            pass_aside(from_prev, (1, k))
        if 0 < k <= n_minus:
            agm[k - 1].wait_recv()
        if k < n_minus:
            piece = slab(from_next, mine, half)
            agm.append(
                send(piece, piece, agm_send_sem.at[k], agm_recv_sem.at[k], {"seq": z_prev})
            )
        if 0 < k <= n_minus:
            pass_aside(from_next, (-1, k))
        if k == 0:
            share_slab(z, 0, width)
        if 0 < k <= n_plus:
            share_slab(from_prev, mine, half)
        if 0 < k <= n_minus:
            share_slab(from_next, mine, half)
        for way, last in ((1, n_plus), (-1, n_minus)):
            if 1 <= k - 1 <= last:
                for copy in ag_side[way, k - 1]:
                    copy.wait_recv()
                share_slab((z + n_z - way * (k - 1)) % n_z, other, half)

    for t in range(2):
        key_row = lax.broadcasted_iota(jnp.int32, (2 * HALF, HALF), 0)
        query_col = lax.broadcasted_iota(jnp.int32, (2 * HALF, HALF), 1)
        own_base = s * 4 + 2 * group[t]
        halo_base = s * 4 - 2 + 6 * group[t]
        key_block = jnp.where(
            key_row < HALF,
            own_base + (key_row >> 7),
            halo_base - 2 + (key_row >> 7),
        )
        early = query_col < BLOCK
        lower = jnp.where(early, first_ref[0, 2 * group[t]], first_ref[0, 2 * group[t] + 1])
        upper = jnp.where(early, last_ref[0, 2 * group[t]], last_ref[0, 2 * group[t] + 1])
        inside = (key_block >= lower) & (key_block < upper)
        bias[t] = jnp.where(inside, 0.0, NEVER)

    def columns(h):
        return pl.ds(pl.multiple_of(h * HDIM, HDIM), HDIM)

    def forward(t, part):
        if part == 0:
            load_q[t].wait()
            load_k[t].wait()
            load_v[t].wait()
        for copy in halo[t, part]:
            copy.wait_recv()

        def head(h, carry):
            cols = columns(h)
            scores = dot(kg[t, :, cols], q[t, :, cols], ((1,), (1,))) * scale + bias[t]
            highest = jnp.max(scores, axis=0, keepdims=True)
            raised = jnp.exp(scores - highest)
            total = jnp.sum(raised, axis=0, keepdims=True)
            p = raised * (1.0 / total)
            probs[t, h] = p
            out_t = dot(vg[t, :, cols], p.astype(BF16), ((0,), (0,)))
            attn_t[pl.ds(pl.multiple_of(h * HDIM, HDIM), HDIM), pl.ds(t * HALF, HALF)] = (
                out_t.astype(BF16)
            )
            attn[pl.ds(t * HALF, HALF), cols] = out_t.T.astype(BF16)
            return carry

        lax.fori_loop(*head_parts[part], head, 0)

    grads = {}

    def backward(t, part):
        def head(h, carry):
            cols = columns(h)
            p = probs[t, h]
            grad_rows = ga[pl.ds(t * HALF, HALF), cols]
            grad_p = dot(vg[t, :, cols], grad_rows, ((1,), (1,)))
            row_term = jnp.sum(p * grad_p, axis=0, keepdims=True)
            grad_s = (p * (grad_p - row_term) * scale).astype(BF16)
            dq_t = dot(kg[t, :, cols], grad_s, ((0,), (0,)))
            dq[t, :, cols] = dq_t.T.astype(BF16)
            dk = dot(grad_s, q[t, :, cols], ((1,), (0,)))
            dv = dot(p.astype(BF16), grad_rows, ((1,), (0,)))
            dk_own[t, :, cols] = dk[:HALF]
            dv_own[t, :, cols] = dv[:HALF]
            dk_send[t, :, cols] = dk[HALF:].astype(BF16)
            dv_send[t, :, cols] = dv[HALF:].astype(BF16)
            return carry

        lax.fori_loop(*head_parts[part], head, 0)
        grads[t, part] = []
        for which, (src, dst) in enumerate(((dk_send, dk_recv), (dv_send, dv_recv))):
            i = (t * 2 + part) * 2 + which
            grads[t, part].append(
                send(
                    src.at[t, :, part_cols(part)], dst.at[t, :, part_cols(part)],
                    grad_send_sem.at[i], grad_recv_sem.at[i], {"seq": partners[t]},
                )
            )

    ag_step(0)
    forward(0, 0)
    ag_step(1)
    forward(0, 1)
    ag_step(2)
    forward(1, 0)
    for k in range(3, n_plus + 1):
        ag_step(k)
    forward(1, 1)
    ag_step(n_plus + 1)

    for copy in load_go:
        copy.wait()
    row_blocks, col_width = hd // HALF, min(512, width)

    def weight_rows(i):
        r = (z * row_blocks // n_z + row_blocks // 2 + i) % row_blocks
        left = attn_t[pl.ds(pl.multiple_of(r * HALF, HALF), HALF), :]

        def tile(n, carry):
            cols = wide(n * col_width, col_width)
            right = go[:, :, cols].reshape(2 * HALF, col_width)
            block = dot(left, right, ((1,), (0,))).astype(BF16)
            wg[pl.ds(r * 8, 8), :, :, cols] = block.reshape(8, CORES, 16, col_width)
            return carry

        lax.fori_loop(0, width // col_width, tile, 0)
        return send(
            wg.at[pl.ds(r * 8, 8), 1 - c], sib_recv.at[pl.ds(r * 8, 8)], rss_send_sem.at[i],
            rss_recv_sem.at[i], {"seq": sibling},
        )

    rss = [weight_rows(i) for i in range(row_blocks)]

    order = []
    for k in range(max(n_plus, n_minus), 0, -1):
        if k <= n_plus:
            order.append((1, k))
        if k <= n_minus:
            order.append((-1, k))
    order.append((1, 0))
    for copy in rss:
        copy.wait_recv()
    rsw = []
    for i, (way, k) in enumerate(order):
        first_row = (z + way * k + n_z) % n_z * n_y

        def add_cores(j, carry, i=i, first_row=first_row):
            for part in range(2):
                cols = wide(other + part * quarter, quarter)
                total = wg[first_row + j, c, :, cols].astype(F32)
                total = total + sib_recv[first_row + j, :, cols].astype(F32)
                side_send[i, part, j] = total.astype(BF16)
            return carry

        lax.fori_loop(0, n_y, add_cores, 0)
        rsw.append(
            [
                send(
                    side_send.at[i, part], side_recv.at[i, part], rsw_send_sem.at[2 * i + part],
                    rsw_recv_sem.at[2 * i + part], {"dp": peer},
                )
                for part, peer in enumerate((x_next, x_prev))
            ]
        )
    rsp, rsm = {}, {}

    def chain(way, k):
        i = order.index((way, k))
        first_row = (z + way * k + n_z) % n_z * n_y
        for copy in rsw[i]:
            copy.wait_recv()
        arrivals = []
        if (way == 1 or k == 0) and k < n_plus:
            rsp[k + 1].wait_recv()
            arrivals.append(plus_recv)
        if (way == -1 or k == 0) and k < n_minus:
            rsm[k + 1].wait_recv()
            arrivals.append(minus_recv)

        def add(j, carry):
            for part in range(2):
                cols = wide(mine + part * quarter, quarter)
                here = pl.ds(part * quarter, quarter)
                total = wg[first_row + j, c, :, cols].astype(F32)
                total = total + sib_recv[first_row + j, :, cols].astype(F32)
                total = total + side_recv[i, part, j].astype(F32)
                for ref in arrivals:
                    total = total + ref[k, j, :, here].astype(F32)
                if k == 0:
                    z_sum[j, :, here] = total
                    y_send[j, :, here] = total.astype(BF16)
                elif way == 1:
                    plus_send[k - 1, j, :, here] = total.astype(BF16)
                else:
                    minus_send[k - 1, j, :, here] = total.astype(BF16)
            return carry

        lax.fori_loop(0, n_y, add, 0)
        if k and way == 1:
            rsp[k] = send(
                plus_send.at[k - 1], plus_recv.at[k - 1], rsp_send_sem.at[k - 1],
                rsp_recv_sem.at[k - 1], {"seq": z_next},
            )
        if k and way == -1:
            rsm[k] = send(
                minus_send.at[k - 1], minus_recv.at[k - 1], rsm_send_sem.at[k - 1],
                rsm_recv_sem.at[k - 1], {"seq": z_prev},
            )

    def chain_level(k):
        if k <= n_plus:
            chain(1, k)
        if 0 < k <= n_minus:
            chain(-1, k)

    for copy in ag_sib:
        copy.wait_recv()

    def grad_tile(i, carry):
        rows = w[pl.ds(i * 8, 8)].reshape(HALF, width)
        tile = dot(go[...].reshape(2 * HALF, width), rows, ((1,), (1,)))
        ga[:, pl.ds(pl.multiple_of(i * HALF, HALF), HALF)] = tile.astype(BF16)
        return carry

    lax.fori_loop(0, row_blocks, grad_tile, 0)

    steps = [(1, 0), (1, 1), (0, 0), (0, 1)]
    for k in range(n_plus, 0, -1):
        chain_level(k)
        if steps:
            backward(*steps.pop(0))
    for step in steps:
        backward(*step)
    chain_level(0)

    stores = []

    def store(src, dst):
        copy = pltpu.make_async_copy(src, dst, store_sem.at[len(stores)])
        copy.start()
        stores.append(copy)

    rsy = [
        send(
            y_send.at[(y + j) % n_y], y_recv.at[j - 1], rsy_send_sem.at[j - 1],
            rsy_recv_sem.at[j - 1], {"seq": peer},
        )
        for j, peer in enumerate(y_peers, 1)
    ]
    for t in range(2):
        store(dq.at[t], dq_hbm.at[token_rows(t)])

    tiles = width // HALF

    def layer_tile(i, carry):
        cols = pl.ds(pl.multiple_of(i * HALF, HALF), HALF)
        right = w[:, :, :, cols].reshape(hd, HALF)
        layer[:, cols] = dot(attn[...], right, ((1,), (0,))).astype(BF16)
        return carry

    lax.fori_loop(0, tiles // 2, layer_tile, 0)

    total = z_sum[y]
    for j, copy in enumerate(rsy):
        copy.wait_recv()
        total = total + y_recv[j].astype(F32)
    x_all[x] = total.astype(BF16)
    rsx = [
        send(
            x_all.at[x], x_all.at[x], rsx_send_sem.at[j], rsx_recv_sem.at[j], {"dp": peer}
        )
        for j, peer in enumerate(x_peers)
    ]
    lax.fori_loop(tiles // 2, tiles, layer_tile, 0)
    for t in range(2):
        store(layer.at[pl.ds(t * HALF, HALF)], layer_hbm.at[token_rows(t)])

    for t in (0, 1):
        for copy in grads[t, 0] + grads[t, 1]:
            copy.wait()
        for own, got, out, hbm in (
            (dk_own, dk_recv, dk_send, dk_hbm), (dv_own, dv_recv, dv_send, dv_hbm)
        ):
            def add_rows(i, carry, own=own, got=got, out=out, t=t):
                rows = pl.ds(pl.multiple_of(i * 32, 32), 32)
                out[t, rows] = (own[t, rows] + got[t, rows].astype(F32)).astype(BF16)
                return carry

            lax.fori_loop(0, HALF // 32, add_rows, 0)
            store(out.at[t], hbm.at[token_rows(t)])

    for copy in rsx:
        copy.wait_recv()
    for parity in range(2):
        total = x_all[parity].astype(F32)
        for j in range(parity + 2, n_x, 2):
            total = total + x_all[j].astype(F32)
        wgrad[:, pl.ds(parity * half, half)] = total * (1.0 / norm)
    store(wgrad, wgrad_hbm)

    waited = sum(grads.values(), [])
    for copy in sent:
        if not any(copy is other for other in waited):
            copy.wait_send()
    for copy in stores:
        copy.wait()


def body(n_seq, n_x, n_y, queries, memory_keys, memory_values, out_weight, grad_out, key_first, key_last):
    rows, hd = queries.shape[1:]
    width = grad_out.shape[2]
    heads = hd // HDIM
    n_z = n_seq // (CORES * n_y)
    n_plus = n_z // 2
    n_minus = n_z - 1 - n_plus
    n_zy = n_z * n_y
    norm = math.sqrt(n_seq * rows)
    sizes = (n_seq, n_x, n_y, n_z, n_plus, n_minus, heads, width, norm)
    vmem, dma = pltpu.VMEM, pltpu.SemaphoreType.DMA
    scratch = [
        vmem((n_zy, CORES, 16, width), BF16),
        vmem((2, HALF, hd), BF16),
        vmem((2, 2 * HALF, hd), BF16),
        vmem((2, 2 * HALF, hd), BF16),
        vmem((2, HALF, width), BF16),
        vmem((2, heads, 2 * HALF, HALF), F32),
        vmem((hd, 2 * HALF), BF16),
        vmem((2 * HALF, hd), BF16),
        vmem((2 * HALF, hd), BF16),
        vmem((2, 2 * HALF, HALF), F32),
        vmem((2, HALF, hd), BF16),
        vmem((2, HALF, hd), F32),
        vmem((2, HALF, hd), F32),
        vmem((2, HALF, hd), BF16),
        vmem((2, HALF, hd), BF16),
        vmem((2, HALF, hd), BF16),
        vmem((2, HALF, hd), BF16),
        vmem((2 * HALF, width), BF16),
        vmem((n_zy, CORES, 16, width), BF16),
        vmem((n_zy, 16, width), BF16),
        vmem((n_z, 2, n_y, 16, width // 4), BF16),
        vmem((n_z, 2, n_y, 16, width // 4), BF16),
        vmem((n_plus, n_y, 16, width // 2), BF16),
        vmem((n_plus, n_y, 16, width // 2), BF16),
        vmem((max(n_minus, 1), n_y, 16, width // 2), BF16),
        vmem((max(n_minus, 1), n_y, 16, width // 2), BF16),
        vmem((n_y, 16, width // 2), F32),
        vmem((n_y, 16, width // 2), BF16),
        vmem((n_y - 1, 16, width // 2), BF16),
        vmem((n_x, 16, width // 2), BF16),
        vmem((16, width), F32),
        dma((9,)),
        dma((9,)),
        dma((8,)), dma((8,)),
        dma((n_y - 1,)), dma((n_y - 1,)),
        dma((n_plus,)), dma((n_plus,)),
        dma((max(n_minus, 1),)), dma((max(n_minus, 1),)),
        dma((2 * n_z,)), dma((2 * n_z,)),
        dma((2 * n_z,)), dma((2 * n_z,)),
        dma((2 * n_z,)), dma((2 * n_z,)),
        dma((hd // HALF,)), dma((hd // HALF,)),
        dma((n_plus,)), dma((n_plus,)),
        dma((max(n_minus, 1),)), dma((max(n_minus, 1),)),
        dma((n_y - 1,)), dma((n_y - 1,)),
        dma((n_x - 1,)), dma((n_x - 1,)),
        dma((8,)), dma((8,)),
    ]
    hbm = pl.BlockSpec(memory_space=pl.ANY)
    smem = pl.BlockSpec(memory_space=pltpu.SMEM)
    layer_out, grad_query, grad_keys, grad_values, weight_grad = pl.pallas_call(
        functools.partial(kernel, sizes),
        out_shape=(
            jax.ShapeDtypeStruct((rows, width), BF16),
            jax.ShapeDtypeStruct((rows, hd), BF16),
            jax.ShapeDtypeStruct((rows, hd), BF16),
            jax.ShapeDtypeStruct((rows, hd), BF16),
            jax.ShapeDtypeStruct((16, width), F32),
        ),
        in_specs=[hbm] * 5 + [smem] * 2,
        out_specs=(hbm,) * 5,
        scratch_shapes=scratch,
        compiler_params=pltpu.CompilerParams(
            collective_id=0, has_side_effects=True, vmem_limit_bytes=60 * 1024 * 1024
        ),
    )(
        queries[0], memory_keys[0], memory_values[0], out_weight, grad_out[0], key_first, key_last
    )
    return (layer_out[None], grad_query[None], grad_keys[None], grad_values[None], weight_grad)


def solution(mesh, n_y=Y_CHIPS):
    return jax.shard_map(
        functools.partial(body, mesh.shape["seq"], mesh.shape["dp"], n_y),
        mesh=mesh,
        in_specs=(
            P("dp", "seq", None),
            P("dp", "seq", None),
            P("dp", "seq", None),
            P("seq", None),
            P("dp", "seq", None),
            P("dp", "seq"),
            P("dp", "seq"),
        ),
        out_specs=(
            P("dp", "seq", None),
            P("dp", "seq", None),
            P("dp", "seq", None),
            P("dp", "seq", None),
            P("seq", None),
        ),
        check_vma=False,
    )
```

```python
import functools
import math

import jax
import jax.numpy as jnp
from jax import lax
from jax.experimental import pallas as pl
from jax.experimental.pallas import tpu as pltpu
from jax.sharding import PartitionSpec as P

HDIM = 128
BLOCK = 128
HALF = 256
CORES = 2
Y_CHIPS = 4
F32 = jnp.float32
BF16 = jnp.bfloat16
NEVER = -1e30
PLAN = (
    "ag0 f00 f01 f10", "wg0 ag1 f11 f02", "wg1 xs0 f03 ag2", "f12 wg2 xs1 zs4",
    "f13 wg3 xs2 ag3", "zs3 ga0 b10 xs3", "zs2 b00 ag4 ga1", "b11 zs1 b01 ga2",
    "b12 zs0 b02 ag5", "ga3 b13 b03",
)
SMALL_PLAN = (
    "ag0 f00 f10 wg0", "ag1 f01 xs0 ag2", "f11 wg1 ga0 zs2", "xs1 b10 b00 zs1",
    "ag3 ga1 b11 zs0", "b01",
)


def dot(a, b, dims):
    return lax.dot_general(a, b, (dims, ((), ())), preferred_element_type=F32)


def kernel(
    sizes,
    q_hbm, k_hbm, v_hbm, shard_hbm, go_hbm, first_ref, last_ref,
    layer_hbm, dq_hbm, dk_hbm, dv_hbm, wgrad_hbm,
    w, q, kg, vg, go, probs, attn_t, attn, ga, bias,
    dq, dk_own, dv_own, dk_send, dv_send, dk_recv, dv_recv, layer,
    wg, sib_recv, side_send, side_recv, plus_send, plus_recv, minus_send, minus_recv,
    z_sum, y_send, y_recv, x_all, wgrad,
    load_sem, store_sem,
    halo_send_sem, halo_recv_sem,
    agy_send_sem, agy_recv_sem, agp_send_sem, agp_recv_sem, agm_send_sem, agm_recv_sem,
    agx_send_sem, agx_recv_sem, ags_send_sem, ags_recv_sem,
    rsw_send_sem, rsw_recv_sem,
    rss_send_sem, rss_recv_sem, rsp_send_sem, rsp_recv_sem, rsm_send_sem, rsm_recv_sem,
    rsy_send_sem, rsy_recv_sem, rsx_send_sem, rsx_recv_sem,
    grad_send_sem, grad_recv_sem,
):
    n_seq, n_x, n_y, n_z, n_plus, n_minus, heads, width, norm = sizes
    scale = 1.0 / math.sqrt(HDIM)
    s = lax.axis_index("seq")
    x = lax.axis_index("dp")
    c = s % CORES
    zy = s // CORES
    y = zy % n_y
    z = zy // n_y

    def at_zy(z_index, y_index, core):
        return (z_index * n_y + y_index) * CORES + core

    sibling = s + 1 - 2 * c
    across = (s + 2 * c - 1 + n_seq) % n_seq
    z_next = at_zy((z + 1) % n_z, y, c)
    z_prev = at_zy((z + n_z - 1) % n_z, y, c)
    y_peers = [at_zy(z, (y + j) % n_y, c) for j in range(1, n_y)]
    x_peers = [(x + j) % n_x for j in range(1, n_x)]
    x_next, x_prev = (x + 1) % n_x, (x + n_x - 1) % n_x
    half, quarter = width // 2, width // 4
    mine, other = (x % 2) * half, (1 - x % 2) * half

    def wide(start, size):
        return pl.ds(pl.multiple_of(start, 128), size)

    pairs = n_z // 2

    def near_first(z_index):
        side = 2 * (z_index % 2) - 1
        steps = (0, side, -side, 2)[:pairs]
        return [(z_index // 2 + step + pairs) % pairs for step in steps]

    near, far = near_first(z), near_first(z)[::-1]

    partners = (sibling, across)
    group = (1 - c, c)

    loads = []

    def load(src, dst):
        copy = pltpu.make_async_copy(src, dst, load_sem.at[len(loads)])
        copy.start()
        loads.append(copy)
        return copy

    def token_rows(t):
        return pl.ds(pl.multiple_of(group[t] * HALF, HALF), HALF)

    load_shard = load(shard_hbm, w.at[zy, c])
    load_q, load_k, load_v, load_go = [], [], [], []
    for t in range(2):
        load_q.append(load(q_hbm.at[token_rows(t)], q.at[t]))
        load_k.append(load(k_hbm.at[token_rows(t)], kg.at[t, pl.ds(0, HALF)]))
        load_v.append(load(v_hbm.at[token_rows(t)], vg.at[t, pl.ds(0, HALF)]))
    for t in range(2):
        load_go.append(load(go_hbm.at[token_rows(t)], go.at[t]))

    barrier = pltpu.get_barrier_semaphore()
    seq_peers = [sibling, across, z_next, z_prev] + y_peers
    for peer in seq_peers:
        pl.semaphore_signal(
            barrier, inc=1, device_id={"seq": peer}, device_id_type=pl.DeviceIdType.MESH
        )
    for peer in x_peers:
        pl.semaphore_signal(
            barrier, inc=1, device_id={"dp": peer}, device_id_type=pl.DeviceIdType.MESH
        )
    pl.semaphore_wait(barrier, len(seq_peers) + len(x_peers))

    sent = []

    def send(src, dst, send_sem, recv_sem, target):
        copy = pltpu.make_async_remote_copy(
            src_ref=src,
            dst_ref=dst,
            send_sem=send_sem,
            recv_sem=recv_sem,
            device_id=target,
            device_id_type=pl.DeviceIdType.MESH,
        )
        copy.start()
        sent.append(copy)
        return copy

    agy = [
        send(
            shard_hbm, w.at[zy, c], agy_send_sem.at[j], agy_recv_sem.at[j], {"seq": peer}
        )
        for j, peer in enumerate(y_peers)
    ]

    def pair_cols(r):
        return pl.ds(pl.multiple_of(r * HALF, HALF), HALF)

    halo = {}
    for t in (1, 0):
        partner_far = near_first(partners[t] // CORES // n_y)[::-1]
        for i, r in enumerate(partner_far):
            halo[t, i] = []
            for which, (src, dst) in enumerate(((k_hbm, kg), (v_hbm, vg))):
                n = (t * pairs + i) * 2 + which
                halo[t, i].append(
                    send(
                        src.at[token_rows(t), pair_cols(r)],
                        dst.at[t, pl.ds(HALF, HALF), pair_cols(r)],
                        halo_send_sem.at[n],
                        halo_recv_sem.at[n],
                        {"seq": partners[t]},
                    )
                )

    def slab(z_index, start, size):
        return w.at[pl.ds(z_index * n_y, n_y), c, :, wide(start, size)]

    ag_sib, ag_side = {}, {}

    def share_slab(key, z_index, start, size):
        i = len(ag_sib)
        piece = slab(z_index, start, size)
        ag_sib[key] = send(
            piece, piece, ags_send_sem.at[i], ags_recv_sem.at[i], {"seq": sibling}
        )

    def pass_aside(z_index, key):
        ag_side[key] = []
        for start, peer in ((mine, x_next), (mine + quarter, x_prev)):
            i = 2 * len(ag_side) - 2 + len(ag_side[key])
            piece = slab(z_index, start, quarter)
            ag_side[key].append(
                send(piece, piece, agx_send_sem.at[i], agx_recv_sem.at[i], {"dp": peer})
            )

    agp, agm = [], []

    def ag_step(k):
        if k == 0:
            load_shard.wait()
            for copy in agy:
                copy.wait_recv()
        from_prev, from_next = (z + n_z - k) % n_z, (z + k) % n_z
        if 0 < k <= n_plus:
            agp[k - 1].wait_recv()
        if k < n_plus:
            piece = slab(from_prev, mine, half)
            agp.append(
                send(piece, piece, agp_send_sem.at[k], agp_recv_sem.at[k], {"seq": z_next})
            )
        if 0 < k <= n_plus:
            pass_aside(from_prev, (1, k))
        if 0 < k <= n_minus:
            agm[k - 1].wait_recv()
        if k < n_minus:
            piece = slab(from_next, mine, half)
            agm.append(
                send(piece, piece, agm_send_sem.at[k], agm_recv_sem.at[k], {"seq": z_prev})
            )
        if 0 < k <= n_minus:
            pass_aside(from_next, (-1, k))
        if k == 0:
            share_slab((0, 0), z, 0, width)
        if 0 < k <= n_plus:
            share_slab((1, k), from_prev, mine, half)
        if 0 < k <= n_minus:
            share_slab((-1, k), from_next, mine, half)
        for way, last in ((1, n_plus), (-1, n_minus)):
            if 1 <= k - 1 <= last:
                for copy in ag_side[way, k - 1]:
                    copy.wait_recv()
                share_slab((way, k - 1, 1), (z + n_z - way * (k - 1)) % n_z, other, half)

    for t in range(2):
        key_row = lax.broadcasted_iota(jnp.int32, (2 * HALF, HALF), 0)
        query_col = lax.broadcasted_iota(jnp.int32, (2 * HALF, HALF), 1)
        own_base = s * 4 + 2 * group[t]
        halo_base = s * 4 - 2 + 6 * group[t]
        key_block = jnp.where(
            key_row < HALF,
            own_base + (key_row >> 7),
            halo_base - 2 + (key_row >> 7),
        )
        early = query_col < BLOCK
        lower = jnp.where(early, first_ref[0, 2 * group[t]], first_ref[0, 2 * group[t] + 1])
        upper = jnp.where(early, last_ref[0, 2 * group[t]], last_ref[0, 2 * group[t] + 1])
        inside = (key_block >= lower) & (key_block < upper)
        bias[t] = jnp.where(inside, 0.0, NEVER)

    def forward(t, i):
        if i == 0:
            load_q[t].wait()
            load_k[t].wait()
            load_v[t].wait()
        for copy in halo[t, i]:
            copy.wait_recv()
        for h in (2 * far[i], 2 * far[i] + 1):
            cols = wide(h * HDIM, HDIM)
            scores = dot(kg[t, :, cols], q[t, :, cols], ((1,), (1,))) * scale + bias[t]
            highest = jnp.max(scores, axis=0, keepdims=True)
            raised = jnp.exp(scores - highest)
            total = jnp.sum(raised, axis=0, keepdims=True)
            p = raised * (1.0 / total)
            probs[t, h] = p
            out_t = dot(vg[t, :, cols], p.astype(BF16), ((0,), (0,)))
            attn_t[cols, pl.ds(t * HALF, HALF)] = out_t.astype(BF16)
            attn[pl.ds(t * HALF, HALF), cols] = out_t.T.astype(BF16)

    grads = []

    def backward(t, i):
        for h in (2 * near[i], 2 * near[i] + 1):
            cols = wide(h * HDIM, HDIM)
            p = probs[t, h]
            grad_rows = ga[pl.ds(t * HALF, HALF), cols]
            grad_p = dot(vg[t, :, cols], grad_rows, ((1,), (1,)))
            row_term = jnp.sum(p * grad_p, axis=0, keepdims=True)
            grad_s = (p * (grad_p - row_term) * scale).astype(BF16)
            dq_t = dot(kg[t, :, cols], grad_s, ((0,), (0,)))
            dq[t, :, cols] = dq_t.T.astype(BF16)
            dk = dot(grad_s, q[t, :, cols], ((1,), (0,)))
            dv = dot(p.astype(BF16), grad_rows, ((1,), (0,)))
            dk_own[t, :, cols] = dk[:HALF]
            dv_own[t, :, cols] = dv[:HALF]
            dk_send[t, :, cols] = dk[HALF:].astype(BF16)
            dv_send[t, :, cols] = dv[HALF:].astype(BF16)
        for which, (src, dst) in enumerate(((dk_send, dk_recv), (dv_send, dv_recv))):
            n = (t * pairs + i) * 2 + which
            piece = pair_cols(near[i])
            copy = send(
                src.at[t, :, piece], dst.at[t, :, piece], grad_send_sem.at[n],
                grad_recv_sem.at[n], {"seq": partners[t]},
            )
            grads.append((copy, t))

    hd = heads * HDIM
    col_width = min(512, width)

    def weight_rows(i):
        r = far[i]
        if i == 0:
            for copy in load_go:
                copy.wait()
        left = attn_t[pair_cols(r), :]

        def tile(n, carry):
            cols = wide(n * col_width, col_width)
            right = go[:, :, cols].reshape(2 * HALF, col_width)
            block = dot(left, right, ((1,), (0,))).astype(BF16)
            wg[pl.ds(r * 8, 8), :, :, cols] = block.reshape(8, CORES, 16, col_width)
            return carry

        lax.fori_loop(0, width // col_width, tile, 0)
        rss.append(
            send(
                wg.at[pl.ds(r * 8, 8), 1 - c], sib_recv.at[pl.ds(r * 8, 8)], rss_send_sem.at[i],
                rss_recv_sem.at[i], {"seq": sibling},
            )
        )

    def grad_attn(i):
        for k in range(i + 2):
            for way in (1, -1):
                for key in ((way, k), (way, k, 1)):
                    if key in ag_sib and key not in ag_here:
                        ag_sib[key].wait_recv()
                        ag_here.append(key)
        if i == 0:
            ag_sib[0, 0].wait_recv()
        rows = w[pl.ds(near[i] * 8, 8)].reshape(HALF, width)
        tile = dot(go[...].reshape(2 * HALF, width), rows, ((1,), (1,)))
        ga[:, pair_cols(near[i])] = tile.astype(BF16)

    rss, ag_here = [], []

    rsw = {}

    def aside(way, k):
        i = len(rsw)
        first_row = (z + way * k + n_z) % n_z * n_y

        def add_cores(j, carry):
            for part in range(2):
                cols = wide(other + part * quarter, quarter)
                total = wg[first_row + j, c, :, cols].astype(F32)
                total = total + sib_recv[first_row + j, :, cols].astype(F32)
                side_send[i, part, j] = total.astype(BF16)
            return carry

        lax.fori_loop(0, n_y, add_cores, 0)
        rsw[way, k] = i, [
            send(
                side_send.at[i, part], side_recv.at[i, part], rsw_send_sem.at[2 * i + part],
                rsw_recv_sem.at[2 * i + part], {"dp": peer},
            )
            for part, peer in enumerate((x_next, x_prev))
        ]

    def aside_level(level):
        rss[level].wait_recv()
        k = n_plus - level
        aside(1, k)
        if k <= n_minus:
            aside(-1, k)
        if k == 1:
            aside(1, 0)

    rsp, rsm = {}, {}

    def chain(way, k):
        i, copies = rsw[way, k]
        first_row = (z + way * k + n_z) % n_z * n_y
        for copy in copies:
            copy.wait_recv()
        arrivals = []
        if (way == 1 or k == 0) and k < n_plus:
            rsp[k + 1].wait_recv()
            arrivals.append(plus_recv)
        if (way == -1 or k == 0) and k < n_minus:
            rsm[k + 1].wait_recv()
            arrivals.append(minus_recv)

        def add(j, carry):
            for part in range(2):
                cols = wide(mine + part * quarter, quarter)
                here = pl.ds(part * quarter, quarter)
                total = wg[first_row + j, c, :, cols].astype(F32)
                total = total + sib_recv[first_row + j, :, cols].astype(F32)
                total = total + side_recv[i, part, j].astype(F32)
                for ref in arrivals:
                    total = total + ref[k, j, :, here].astype(F32)
                if k == 0:
                    z_sum[j, :, here] = total
                    y_send[j, :, here] = total.astype(BF16)
                elif way == 1:
                    plus_send[k - 1, j, :, here] = total.astype(BF16)
                else:
                    minus_send[k - 1, j, :, here] = total.astype(BF16)
            return carry

        lax.fori_loop(0, n_y, add, 0)
        if k and way == 1:
            rsp[k] = send(
                plus_send.at[k - 1], plus_recv.at[k - 1], rsp_send_sem.at[k - 1],
                rsp_recv_sem.at[k - 1], {"seq": z_next},
            )
        if k and way == -1:
            rsm[k] = send(
                minus_send.at[k - 1], minus_recv.at[k - 1], rsm_send_sem.at[k - 1],
                rsm_recv_sem.at[k - 1], {"seq": z_prev},
            )

    def chain_level(k):
        if k <= n_plus:
            chain(1, k)
        if 0 < k <= n_minus:
            chain(-1, k)

    plan = PLAN if n_z == 8 else SMALL_PLAN
    steps = {
        "ag": ag_step, "f0": functools.partial(forward, 0), "f1": functools.partial(forward, 1),
        "wg": weight_rows, "xs": aside_level, "zs": chain_level, "ga": grad_attn,
        "b0": functools.partial(backward, 0), "b1": functools.partial(backward, 1),
    }
    for item in " ".join(plan).split():
        steps[item[:2]](int(item[2:]))

    stores = []

    def store(src, dst):
        copy = pltpu.make_async_copy(src, dst, store_sem.at[len(stores)])
        copy.start()
        stores.append(copy)

    rsy = [
        send(
            y_send.at[(y + j) % n_y], y_recv.at[j - 1], rsy_send_sem.at[j - 1],
            rsy_recv_sem.at[j - 1], {"seq": peer},
        )
        for j, peer in enumerate(y_peers, 1)
    ]
    for t in range(2):
        store(dq.at[t], dq_hbm.at[token_rows(t)])

    tiles = width // HALF

    def layer_tile(i, carry):
        cols = pl.ds(pl.multiple_of(i * HALF, HALF), HALF)
        right = w[:, :, :, cols].reshape(hd, HALF)
        layer[:, cols] = dot(attn[...], right, ((1,), (0,))).astype(BF16)
        return carry

    lax.fori_loop(0, tiles // 2, layer_tile, 0)

    total = z_sum[y]
    for j, copy in enumerate(rsy):
        copy.wait_recv()
        total = total + y_recv[j].astype(F32)
    x_all[x] = total.astype(BF16)
    rsx = [
        send(
            x_all.at[x], x_all.at[x], rsx_send_sem.at[j], rsx_recv_sem.at[j], {"dp": peer}
        )
        for j, peer in enumerate(x_peers)
    ]
    lax.fori_loop(tiles // 2, tiles, layer_tile, 0)
    for t in range(2):
        store(layer.at[pl.ds(t * HALF, HALF)], layer_hbm.at[token_rows(t)])

    grads_of = {t: [copy for copy, slot in grads if slot == t] for t in range(2)}
    for t in (0, 1):
        for copy in grads_of[t]:
            copy.wait()
        for own, got, out, hbm in (
            (dk_own, dk_recv, dk_send, dk_hbm), (dv_own, dv_recv, dv_send, dv_hbm)
        ):
            def add_rows(i, carry, own=own, got=got, out=out, t=t):
                rows = pl.ds(pl.multiple_of(i * 32, 32), 32)
                out[t, rows] = (own[t, rows] + got[t, rows].astype(F32)).astype(BF16)
                return carry

            lax.fori_loop(0, HALF // 32, add_rows, 0)
            store(out.at[t], hbm.at[token_rows(t)])

    for copy in rsx:
        copy.wait_recv()
    for parity in range(2):
        total = x_all[parity].astype(F32)
        for j in range(parity + 2, n_x, 2):
            total = total + x_all[j].astype(F32)
        wgrad[:, pl.ds(parity * half, half)] = total * (1.0 / norm)
    store(wgrad, wgrad_hbm)

    waited = [copy for copy, _ in grads]
    for copy in sent:
        if not any(copy is other for other in waited):
            copy.wait_send()
    for copy in stores:
        copy.wait()


def body(n_seq, n_x, n_y, queries, memory_keys, memory_values, out_weight, grad_out, key_first, key_last):
    rows, hd = queries.shape[1:]
    width = grad_out.shape[2]
    heads = hd // HDIM
    n_z = n_seq // (CORES * n_y)
    n_plus = n_z // 2
    n_minus = n_z - 1 - n_plus
    n_zy = n_z * n_y
    norm = math.sqrt(n_seq * rows)
    sizes = (n_seq, n_x, n_y, n_z, n_plus, n_minus, heads, width, norm)
    vmem, dma = pltpu.VMEM, pltpu.SemaphoreType.DMA
    scratch = [
        vmem((n_zy, CORES, 16, width), BF16),
        vmem((2, HALF, hd), BF16),
        vmem((2, 2 * HALF, hd), BF16),
        vmem((2, 2 * HALF, hd), BF16),
        vmem((2, HALF, width), BF16),
        vmem((2, heads, 2 * HALF, HALF), F32),
        vmem((hd, 2 * HALF), BF16),
        vmem((2 * HALF, hd), BF16),
        vmem((2 * HALF, hd), BF16),
        vmem((2, 2 * HALF, HALF), F32),
        vmem((2, HALF, hd), BF16),
        vmem((2, HALF, hd), F32),
        vmem((2, HALF, hd), F32),
        vmem((2, HALF, hd), BF16),
        vmem((2, HALF, hd), BF16),
        vmem((2, HALF, hd), BF16),
        vmem((2, HALF, hd), BF16),
        vmem((2 * HALF, width), BF16),
        vmem((n_zy, CORES, 16, width), BF16),
        vmem((n_zy, 16, width), BF16),
        vmem((n_z, 2, n_y, 16, width // 4), BF16),
        vmem((n_z, 2, n_y, 16, width // 4), BF16),
        vmem((n_plus, n_y, 16, width // 2), BF16),
        vmem((n_plus, n_y, 16, width // 2), BF16),
        vmem((max(n_minus, 1), n_y, 16, width // 2), BF16),
        vmem((max(n_minus, 1), n_y, 16, width // 2), BF16),
        vmem((n_y, 16, width // 2), F32),
        vmem((n_y, 16, width // 2), BF16),
        vmem((n_y - 1, 16, width // 2), BF16),
        vmem((n_x, 16, width // 2), BF16),
        vmem((16, width), F32),
        dma((9,)),
        dma((9,)),
        dma((2 * n_z,)), dma((2 * n_z,)),
        dma((n_y - 1,)), dma((n_y - 1,)),
        dma((n_plus,)), dma((n_plus,)),
        dma((max(n_minus, 1),)), dma((max(n_minus, 1),)),
        dma((2 * n_z,)), dma((2 * n_z,)),
        dma((2 * n_z,)), dma((2 * n_z,)),
        dma((2 * n_z,)), dma((2 * n_z,)),
        dma((hd // HALF,)), dma((hd // HALF,)),
        dma((n_plus,)), dma((n_plus,)),
        dma((max(n_minus, 1),)), dma((max(n_minus, 1),)),
        dma((n_y - 1,)), dma((n_y - 1,)),
        dma((n_x - 1,)), dma((n_x - 1,)),
        dma((2 * n_z,)), dma((2 * n_z,)),
    ]
    hbm = pl.BlockSpec(memory_space=pl.ANY)
    smem = pl.BlockSpec(memory_space=pltpu.SMEM)
    layer_out, grad_query, grad_keys, grad_values, weight_grad = pl.pallas_call(
        functools.partial(kernel, sizes),
        out_shape=(
            jax.ShapeDtypeStruct((rows, width), BF16),
            jax.ShapeDtypeStruct((rows, hd), BF16),
            jax.ShapeDtypeStruct((rows, hd), BF16),
            jax.ShapeDtypeStruct((rows, hd), BF16),
            jax.ShapeDtypeStruct((16, width), F32),
        ),
        in_specs=[hbm] * 5 + [smem] * 2,
        out_specs=(hbm,) * 5,
        scratch_shapes=scratch,
        compiler_params=pltpu.CompilerParams(
            collective_id=0, has_side_effects=True, vmem_limit_bytes=60 * 1024 * 1024
        ),
    )(
        queries[0], memory_keys[0], memory_values[0], out_weight, grad_out[0], key_first, key_last
    )
    return (layer_out[None], grad_query[None], grad_keys[None], grad_values[None], weight_grad)


def solution(mesh, n_y=Y_CHIPS):
    return jax.shard_map(
        functools.partial(body, mesh.shape["seq"], mesh.shape["dp"], n_y),
        mesh=mesh,
        in_specs=(
            P("dp", "seq", None),
            P("dp", "seq", None),
            P("dp", "seq", None),
            P("seq", None),
            P("dp", "seq", None),
            P("dp", "seq"),
            P("dp", "seq"),
        ),
        out_specs=(
            P("dp", "seq", None),
            P("dp", "seq", None),
            P("dp", "seq", None),
            P("dp", "seq", None),
            P("seq", None),
        ),
        check_vma=False,
    )
```

```python
import functools
import math

import jax
import jax.numpy as jnp
from jax import lax
from jax.experimental import pallas as pl
from jax.experimental.pallas import tpu as pltpu
from jax.sharding import PartitionSpec as P

HDIM = 128
BLOCK = 128
HALF = 256
CORES = 2
Y_CHIPS = 4
F32 = jnp.float32
BF16 = jnp.bfloat16
NEVER = -1e30
LAYER_PARTS = 4
PLAN = (
    "ag0 f00 f01 f10", "wg0 ag1 f11 f02", "wg1 xs0 f03 f12", "ag2 wg2 xs1 zs4",
    "f13 wg3 xs2 ag3", "ga0 zs3 b10 xs3", "b00 zs2 ag4 ga1", "b11 b01 zs1 ga2",
    "b12 b02 ag5 zs0", "ys0 ga3 kp0 b13", "yx0 b03 xx0 gs0", "gs1",
)
SMALL_PLAN = (
    "ag0 f00 f10 wg0", "ag1 f01 xs0 ag2", "f11 wg1 ga0 zs2", "xs1 b10 b00 zs1",
    "ag3 ga1 kp0 b11", "zs0 ys0 b01 yx0", "gs0 gs1 xx0",
)


def dot(a, b, dims):
    return lax.dot_general(a, b, (dims, ((), ())), preferred_element_type=F32)


def kernel(
    sizes,
    q_hbm, k_hbm, v_hbm, shard_hbm, go_hbm, first_ref, last_ref,
    attn_hbm, w_hbm, dq_hbm, dk_hbm, dv_hbm, wgrad_hbm,
    w, q, kg, vg, go, probs, attn_t, attn, ga, bias,
    dq, dk_own, dv_own, dk_send, dv_send, dk_recv, dv_recv,
    wg, sib_recv, side_send, side_recv, plus_send, plus_recv, minus_send, minus_recv,
    z_sum, y_send, y_recv, x_all, wgrad,
    load_sem, store_sem,
    halo_send_sem, halo_recv_sem,
    agy_send_sem, agy_recv_sem, agp_send_sem, agp_recv_sem, agm_send_sem, agm_recv_sem,
    agx_send_sem, agx_recv_sem, ags_send_sem, ags_recv_sem,
    rsw_send_sem, rsw_recv_sem,
    rss_send_sem, rss_recv_sem, rsp_send_sem, rsp_recv_sem, rsm_send_sem, rsm_recv_sem,
    rsy_send_sem, rsy_recv_sem, rsx_send_sem, rsx_recv_sem,
    grad_send_sem, grad_recv_sem,
):
    n_seq, n_x, n_y, n_z, n_plus, n_minus, heads, width, norm = sizes
    scale = 1.0 / math.sqrt(HDIM)
    s = lax.axis_index("seq")
    x = lax.axis_index("dp")
    c = s % CORES
    zy = s // CORES
    y = zy % n_y
    z = zy // n_y

    def at_zy(z_index, y_index, core):
        return (z_index * n_y + y_index) * CORES + core

    sibling = s + 1 - 2 * c
    across = (s + 2 * c - 1 + n_seq) % n_seq
    z_next = at_zy((z + 1) % n_z, y, c)
    z_prev = at_zy((z + n_z - 1) % n_z, y, c)
    y_peers = [at_zy(z, (y + j) % n_y, c) for j in range(1, n_y)]
    x_peers = [(x + j) % n_x for j in range(1, n_x)]
    x_next, x_prev = (x + 1) % n_x, (x + n_x - 1) % n_x
    half, quarter = width // 2, width // 4
    mine, other = (x % 2) * half, (1 - x % 2) * half

    def wide(start, size):
        return pl.ds(pl.multiple_of(start, 128), size)

    pairs = n_z // 2

    def near_first(z_index):
        side = 2 * (z_index % 2) - 1
        steps = (0, side, -side, 2)[:pairs]
        return [(z_index // 2 + step + pairs) % pairs for step in steps]

    near, far = near_first(z), near_first(z)[::-1]

    partners = (sibling, across)
    group = (1 - c, c)

    loads = []

    def load(src, dst):
        copy = pltpu.make_async_copy(src, dst, load_sem.at[len(loads)])
        copy.start()
        loads.append(copy)
        return copy

    def token_rows(t):
        return pl.ds(pl.multiple_of(group[t] * HALF, HALF), HALF)

    load_shard = load(shard_hbm, w.at[zy, c])
    load_q, load_k, load_v, load_go = [], [], [], []
    for t in range(2):
        load_q.append(load(q_hbm.at[token_rows(t)], q.at[t]))
        load_k.append(load(k_hbm.at[token_rows(t)], kg.at[t, pl.ds(0, HALF)]))
        load_v.append(load(v_hbm.at[token_rows(t)], vg.at[t, pl.ds(0, HALF)]))
    for t in range(2):
        load_go.append(load(go_hbm.at[token_rows(t)], go.at[t]))

    barrier = pltpu.get_barrier_semaphore()
    seq_peers = [sibling, across, z_next, z_prev] + y_peers
    for peer in seq_peers:
        pl.semaphore_signal(
            barrier, inc=1, device_id={"seq": peer}, device_id_type=pl.DeviceIdType.MESH
        )
    for peer in x_peers:
        pl.semaphore_signal(
            barrier, inc=1, device_id={"dp": peer}, device_id_type=pl.DeviceIdType.MESH
        )
    pl.semaphore_wait(barrier, len(seq_peers) + len(x_peers))

    sent = []

    def send(src, dst, send_sem, recv_sem, target):
        copy = pltpu.make_async_remote_copy(
            src_ref=src,
            dst_ref=dst,
            send_sem=send_sem,
            recv_sem=recv_sem,
            device_id=target,
            device_id_type=pl.DeviceIdType.MESH,
        )
        copy.start()
        sent.append(copy)
        return copy

    agy = [
        send(
            shard_hbm, w.at[zy, c], agy_send_sem.at[j], agy_recv_sem.at[j], {"seq": peer}
        )
        for j, peer in enumerate(y_peers)
    ]

    def pair_cols(r):
        return pl.ds(pl.multiple_of(r * HALF, HALF), HALF)

    halo = {}
    for t in (1, 0):
        partner_far = near_first(partners[t] // CORES // n_y)[::-1]
        for i, r in enumerate(partner_far):
            halo[t, i] = []
            for which, (src, dst) in enumerate(((k_hbm, kg), (v_hbm, vg))):
                n = (t * pairs + i) * 2 + which
                halo[t, i].append(
                    send(
                        src.at[token_rows(t), pair_cols(r)],
                        dst.at[t, pl.ds(HALF, HALF), pair_cols(r)],
                        halo_send_sem.at[n],
                        halo_recv_sem.at[n],
                        {"seq": partners[t]},
                    )
                )

    def slab(z_index, start, size):
        return w.at[pl.ds(z_index * n_y, n_y), c, :, wide(start, size)]

    ag_sib, ag_side = {}, {}

    def share_slab(key, z_index, start, size):
        i = len(ag_sib)
        piece = slab(z_index, start, size)
        ag_sib[key] = send(
            piece, piece, ags_send_sem.at[i], ags_recv_sem.at[i], {"seq": sibling}
        )

    def pass_aside(z_index, key):
        ag_side[key] = []
        for start, peer in ((mine, x_next), (mine + quarter, x_prev)):
            i = 2 * len(ag_side) - 2 + len(ag_side[key])
            piece = slab(z_index, start, quarter)
            ag_side[key].append(
                send(piece, piece, agx_send_sem.at[i], agx_recv_sem.at[i], {"dp": peer})
            )

    agp, agm = [], []

    def ag_step(k):
        if k == 0:
            load_shard.wait()
            for copy in agy:
                copy.wait_recv()
        from_prev, from_next = (z + n_z - k) % n_z, (z + k) % n_z
        if 0 < k <= n_plus:
            agp[k - 1].wait_recv()
        if k < n_plus:
            piece = slab(from_prev, mine, half)
            agp.append(
                send(piece, piece, agp_send_sem.at[k], agp_recv_sem.at[k], {"seq": z_next})
            )
        if 0 < k <= n_plus:
            pass_aside(from_prev, (1, k))
        if 0 < k <= n_minus:
            agm[k - 1].wait_recv()
        if k < n_minus:
            piece = slab(from_next, mine, half)
            agm.append(
                send(piece, piece, agm_send_sem.at[k], agm_recv_sem.at[k], {"seq": z_prev})
            )
        if 0 < k <= n_minus:
            pass_aside(from_next, (-1, k))
        if k == 0:
            share_slab((0, 0), z, 0, width)
        if 0 < k <= n_plus:
            share_slab((1, k), from_prev, mine, half)
        if 0 < k <= n_minus:
            share_slab((-1, k), from_next, mine, half)
        for way, last in ((1, n_plus), (-1, n_minus)):
            if 1 <= k - 1 <= last:
                for copy in ag_side[way, k - 1]:
                    copy.wait_recv()
                share_slab((way, k - 1, 1), (z + n_z - way * (k - 1)) % n_z, other, half)

    for t in range(2):
        key_row = lax.broadcasted_iota(jnp.int32, (2 * HALF, HALF), 0)
        query_col = lax.broadcasted_iota(jnp.int32, (2 * HALF, HALF), 1)
        own_base = s * 4 + 2 * group[t]
        halo_base = s * 4 - 2 + 6 * group[t]
        key_block = jnp.where(
            key_row < HALF,
            own_base + (key_row >> 7),
            halo_base - 2 + (key_row >> 7),
        )
        early = query_col < BLOCK
        lower = jnp.where(early, first_ref[0, 2 * group[t]], first_ref[0, 2 * group[t] + 1])
        upper = jnp.where(early, last_ref[0, 2 * group[t]], last_ref[0, 2 * group[t] + 1])
        inside = (key_block >= lower) & (key_block < upper)
        bias[t] = jnp.where(inside, 0.0, NEVER)

    def forward(t, i):
        if i == 0:
            load_q[t].wait()
            load_k[t].wait()
            load_v[t].wait()
        for copy in halo[t, i]:
            copy.wait_recv()
        for h in (2 * far[i], 2 * far[i] + 1):
            cols = wide(h * HDIM, HDIM)
            scores = dot(kg[t, :, cols], q[t, :, cols], ((1,), (1,))) * scale + bias[t]
            highest = jnp.max(scores, axis=0, keepdims=True)
            raised = jnp.exp(scores - highest)
            total = jnp.sum(raised, axis=0, keepdims=True)
            p = raised * (1.0 / total)
            probs[t, h] = p
            out_t = dot(vg[t, :, cols], p.astype(BF16), ((0,), (0,)))
            attn_t[cols, pl.ds(t * HALF, HALF)] = out_t.astype(BF16)
            attn[pl.ds(t * HALF, HALF), cols] = out_t.T.astype(BF16)

    grads = []

    def backward(t, i):
        for h in (2 * near[i], 2 * near[i] + 1):
            cols = wide(h * HDIM, HDIM)
            p = probs[t, h]
            grad_rows = ga[pl.ds(t * HALF, HALF), cols]
            grad_p = dot(vg[t, :, cols], grad_rows, ((1,), (1,)))
            row_term = jnp.sum(p * grad_p, axis=0, keepdims=True)
            grad_s = (p * (grad_p - row_term) * scale).astype(BF16)
            dq_t = dot(kg[t, :, cols], grad_s, ((0,), (0,)))
            dq[t, :, cols] = dq_t.T.astype(BF16)
            dk = dot(grad_s, q[t, :, cols], ((1,), (0,)))
            dv = dot(p.astype(BF16), grad_rows, ((1,), (0,)))
            dk_own[t, :, cols] = dk[:HALF]
            dv_own[t, :, cols] = dv[:HALF]
            dk_send[t, :, cols] = dk[HALF:].astype(BF16)
            dv_send[t, :, cols] = dv[HALF:].astype(BF16)
        for which, (src, dst) in enumerate(((dk_send, dk_recv), (dv_send, dv_recv))):
            n = (t * pairs + i) * 2 + which
            piece = pair_cols(near[i])
            copy = send(
                src.at[t, :, piece], dst.at[t, :, piece], grad_send_sem.at[n],
                grad_recv_sem.at[n], {"seq": partners[t]},
            )
            grads.append((copy, t))

    hd = heads * HDIM
    col_width = min(512, width)

    def weight_rows(i):
        r = far[i]
        if i == 0:
            for copy in load_go:
                copy.wait()
        left = attn_t[pair_cols(r), :]

        def tile(n, carry):
            cols = wide(n * col_width, col_width)
            right = go[:, :, cols].reshape(2 * HALF, col_width)
            block = dot(left, right, ((1,), (0,))).astype(BF16)
            wg[pl.ds(r * 8, 8), :, :, cols] = block.reshape(8, CORES, 16, col_width)
            return carry

        lax.fori_loop(0, width // col_width, tile, 0)
        rss.append(
            send(
                wg.at[pl.ds(r * 8, 8), 1 - c], sib_recv.at[pl.ds(r * 8, 8)], rss_send_sem.at[i],
                rss_recv_sem.at[i], {"seq": sibling},
            )
        )

    def grad_attn(i):
        for k in range(i + 2):
            for way in (1, -1):
                for key in ((way, k), (way, k, 1)):
                    if key in ag_sib and key not in ag_here:
                        ag_sib[key].wait_recv()
                        ag_here.append(key)
        if i == 0:
            ag_sib[0, 0].wait_recv()
        rows = w[pl.ds(near[i] * 8, 8)].reshape(HALF, width)
        tile = dot(go[...].reshape(2 * HALF, width), rows, ((1,), (1,)))
        ga[:, pair_cols(near[i])] = tile.astype(BF16)

    rss, ag_here = [], []

    rsw = {}

    def aside(way, k):
        i = len(rsw)
        first_row = (z + way * k + n_z) % n_z * n_y

        def add_cores(j, carry):
            for part in range(2):
                cols = wide(other + part * quarter, quarter)
                total = wg[first_row + j, c, :, cols].astype(F32)
                total = total + sib_recv[first_row + j, :, cols].astype(F32)
                side_send[i, part, j] = total.astype(BF16)
            return carry

        lax.fori_loop(0, n_y, add_cores, 0)
        rsw[way, k] = i, [
            send(
                side_send.at[i, part], side_recv.at[i, part], rsw_send_sem.at[2 * i + part],
                rsw_recv_sem.at[2 * i + part], {"dp": peer},
            )
            for part, peer in enumerate((x_next, x_prev))
        ]

    def aside_level(level):
        rss[level].wait_recv()
        k = n_plus - level
        aside(1, k)
        if k <= n_minus:
            aside(-1, k)
        if k == 1:
            aside(1, 0)

    rsp, rsm = {}, {}

    def chain(way, k):
        i, copies = rsw[way, k]
        first_row = (z + way * k + n_z) % n_z * n_y
        for copy in copies:
            copy.wait_recv()
        arrivals = []
        if (way == 1 or k == 0) and k < n_plus:
            rsp[k + 1].wait_recv()
            arrivals.append(plus_recv)
        if (way == -1 or k == 0) and k < n_minus:
            rsm[k + 1].wait_recv()
            arrivals.append(minus_recv)

        def add(j, carry):
            for part in range(2):
                cols = wide(mine + part * quarter, quarter)
                here = pl.ds(part * quarter, quarter)
                total = wg[first_row + j, c, :, cols].astype(F32)
                total = total + sib_recv[first_row + j, :, cols].astype(F32)
                total = total + side_recv[i, part, j].astype(F32)
                for ref in arrivals:
                    total = total + ref[k, j, :, here].astype(F32)
                if k == 0:
                    z_sum[j, :, here] = total
                    y_send[j, :, here] = total.astype(BF16)
                elif way == 1:
                    plus_send[k - 1, j, :, here] = total.astype(BF16)
                else:
                    minus_send[k - 1, j, :, here] = total.astype(BF16)
            return carry

        lax.fori_loop(0, n_y, add, 0)
        if k and way == 1:
            rsp[k] = send(
                plus_send.at[k - 1], plus_recv.at[k - 1], rsp_send_sem.at[k - 1],
                rsp_recv_sem.at[k - 1], {"seq": z_next},
            )
        if k and way == -1:
            rsm[k] = send(
                minus_send.at[k - 1], minus_recv.at[k - 1], rsm_send_sem.at[k - 1],
                rsm_recv_sem.at[k - 1], {"seq": z_prev},
            )

    def chain_level(k):
        if k <= n_plus:
            chain(1, k)
        if 0 < k <= n_minus:
            chain(-1, k)

    stores = []

    def store(src, dst):
        copy = pltpu.make_async_copy(src, dst, store_sem.at[len(stores)])
        copy.start()
        stores.append(copy)

    rsy, rsx = [], []

    def along_y(_):
        for j, peer in enumerate(y_peers, 1):
            rsy.append(
                send(
                    y_send.at[(y + j) % n_y], y_recv.at[j - 1], rsy_send_sem.at[j - 1],
                    rsy_recv_sem.at[j - 1], {"seq": peer},
                )
            )

    def along_x(_):
        total = z_sum[y]
        for j, copy in enumerate(rsy):
            copy.wait_recv()
            total = total + y_recv[j].astype(F32)
        x_all[x] = total.astype(BF16)
        for j, peer in enumerate(x_peers):
            rsx.append(
                send(
                    x_all.at[x], x_all.at[x], rsx_send_sem.at[j], rsx_recv_sem.at[j],
                    {"dp": peer},
                )
            )

    def last_sum(_):
        for copy in rsx:
            copy.wait_recv()
        for parity in range(2):
            total = x_all[parity].astype(F32)
            for j in range(parity + 2, n_x, 2):
                total = total + x_all[j].astype(F32)
            wgrad[:, pl.ds(parity * half, half)] = total * (1.0 / norm)
        store(wgrad, wgrad_hbm)

    def keep(_):
        for t in range(2):
            store(attn.at[pl.ds(t * HALF, HALF)], attn_hbm.at[token_rows(t)])
        store(w, w_hbm)

    def grad_sum(t):
        store(dq.at[t], dq_hbm.at[token_rows(t)])
        for copy, slot in grads:
            if slot == t:
                copy.wait()
        for own, got, out, hbm in (
            (dk_own, dk_recv, dk_send, dk_hbm), (dv_own, dv_recv, dv_send, dv_hbm)
        ):
            def add_rows(i, carry, own=own, got=got, out=out):
                rows = pl.ds(pl.multiple_of(i * 32, 32), 32)
                out[t, rows] = (own[t, rows] + got[t, rows].astype(F32)).astype(BF16)
                return carry

            lax.fori_loop(0, HALF // 32, add_rows, 0)
            store(out.at[t], hbm.at[token_rows(t)])

    plan = PLAN if n_z == 8 else SMALL_PLAN
    steps = {
        "ag": ag_step, "f0": functools.partial(forward, 0), "f1": functools.partial(forward, 1),
        "wg": weight_rows, "xs": aside_level, "zs": chain_level, "ga": grad_attn,
        "b0": functools.partial(backward, 0), "b1": functools.partial(backward, 1),
        "ys": along_y, "yx": along_x, "xx": last_sum, "kp": keep, "gs": grad_sum,
    }
    for item in " ".join(plan).split():
        steps[item[:2]](int(item[2:]))

    waited = [copy for copy, _ in grads]
    for copy in sent:
        if not any(copy is other for other in waited):
            copy.wait_send()
    for copy in stores:
        copy.wait()


def layer_kernel(
    attn_hbm, w_hbm, dq_in, dk_in, dv_in, wgrad_in,
    layer_hbm, dq_out, dk_out, dv_out, wgrad_out,
    attn, w, layer, dq, dk, dv, wgrad,
    load_sem, store_sem, in_sem, out_sem,
):
    hd, width = attn.shape[1], layer.shape[1]
    size = width // LAYER_PARTS
    parts = [pl.ds(n * size, size) for n in range(LAYER_PARTS)]
    loads = [pltpu.make_async_copy(attn_hbm, attn, load_sem.at[LAYER_PARTS])]
    for n, cols in enumerate(parts):
        loads.append(
            pltpu.make_async_copy(
                w_hbm.at[:, :, :, cols], w.at[:, :, :, cols], load_sem.at[n]
            )
        )
    moved = (
        (dq_in, dq, dq_out), (dk_in, dk, dk_out), (dv_in, dv, dv_out), (wgrad_in, wgrad, wgrad_out)
    )
    moves = [
        pltpu.make_async_copy(source, held, in_sem.at[n])
        for n, (source, held, _) in enumerate(moved)
    ]
    for copy in loads + moves:
        copy.start()
    stores = []
    loads[0].wait()
    for n, cols in enumerate(parts):
        loads[n + 1].wait()
        right = w[:, :, :, cols].reshape(hd, size)
        layer[:, cols] = dot(attn[...], right, ((1,), (0,))).astype(BF16)
        stores.append(
            pltpu.make_async_copy(layer.at[:, cols], layer_hbm.at[:, cols], store_sem.at[n])
        )
        stores[-1].start()
        if n < len(moved):
            _, held, target = moved[n]
            moves[n].wait()
            stores.append(pltpu.make_async_copy(held, target, out_sem.at[n]))
            stores[-1].start()
    for copy in stores:
        copy.wait()


def body(n_seq, n_x, n_y, queries, memory_keys, memory_values, out_weight, grad_out, key_first, key_last):
    rows, hd = queries.shape[1:]
    width = grad_out.shape[2]
    heads = hd // HDIM
    n_z = n_seq // (CORES * n_y)
    n_plus = n_z // 2
    n_minus = n_z - 1 - n_plus
    n_zy = n_z * n_y
    norm = math.sqrt(n_seq * rows)
    sizes = (n_seq, n_x, n_y, n_z, n_plus, n_minus, heads, width, norm)
    vmem, dma = pltpu.VMEM, pltpu.SemaphoreType.DMA
    scratch = [
        vmem((n_zy, CORES, 16, width), BF16),
        vmem((2, HALF, hd), BF16),
        vmem((2, 2 * HALF, hd), BF16),
        vmem((2, 2 * HALF, hd), BF16),
        vmem((2, HALF, width), BF16),
        vmem((2, heads, 2 * HALF, HALF), F32),
        vmem((hd, 2 * HALF), BF16),
        vmem((2 * HALF, hd), BF16),
        vmem((2 * HALF, hd), BF16),
        vmem((2, 2 * HALF, HALF), F32),
        vmem((2, HALF, hd), BF16),
        vmem((2, HALF, hd), F32),
        vmem((2, HALF, hd), F32),
        vmem((2, HALF, hd), BF16),
        vmem((2, HALF, hd), BF16),
        vmem((2, HALF, hd), BF16),
        vmem((2, HALF, hd), BF16),
        vmem((n_zy, CORES, 16, width), BF16),
        vmem((n_zy, 16, width), BF16),
        vmem((n_z, 2, n_y, 16, width // 4), BF16),
        vmem((n_z, 2, n_y, 16, width // 4), BF16),
        vmem((n_plus, n_y, 16, width // 2), BF16),
        vmem((n_plus, n_y, 16, width // 2), BF16),
        vmem((max(n_minus, 1), n_y, 16, width // 2), BF16),
        vmem((max(n_minus, 1), n_y, 16, width // 2), BF16),
        vmem((n_y, 16, width // 2), F32),
        vmem((n_y, 16, width // 2), BF16),
        vmem((n_y - 1, 16, width // 2), BF16),
        vmem((n_x, 16, width // 2), BF16),
        vmem((16, width), F32),
        dma((9,)),
        dma((10,)),
        dma((2 * n_z,)), dma((2 * n_z,)),
        dma((n_y - 1,)), dma((n_y - 1,)),
        dma((n_plus,)), dma((n_plus,)),
        dma((max(n_minus, 1),)), dma((max(n_minus, 1),)),
        dma((2 * n_z,)), dma((2 * n_z,)),
        dma((2 * n_z,)), dma((2 * n_z,)),
        dma((2 * n_z,)), dma((2 * n_z,)),
        dma((hd // HALF,)), dma((hd // HALF,)),
        dma((n_plus,)), dma((n_plus,)),
        dma((max(n_minus, 1),)), dma((max(n_minus, 1),)),
        dma((n_y - 1,)), dma((n_y - 1,)),
        dma((n_x - 1,)), dma((n_x - 1,)),
        dma((2 * n_z,)), dma((2 * n_z,)),
    ]
    hbm = pl.BlockSpec(memory_space=pl.ANY)
    smem = pl.BlockSpec(memory_space=pltpu.SMEM)
    attn, weight, *grads = pl.pallas_call(
        functools.partial(kernel, sizes),
        out_shape=(
            jax.ShapeDtypeStruct((rows, hd), BF16),
            jax.ShapeDtypeStruct((n_zy, CORES, 16, width), BF16),
            jax.ShapeDtypeStruct((rows, hd), BF16),
            jax.ShapeDtypeStruct((rows, hd), BF16),
            jax.ShapeDtypeStruct((rows, hd), BF16),
            jax.ShapeDtypeStruct((16, width), F32),
        ),
        in_specs=[hbm] * 5 + [smem] * 2,
        out_specs=(hbm,) * 6,
        scratch_shapes=scratch,
        compiler_params=pltpu.CompilerParams(
            collective_id=0, has_side_effects=True, vmem_limit_bytes=60 * 1024 * 1024
        ),
    )(
        queries[0], memory_keys[0], memory_values[0], out_weight, grad_out[0], key_first, key_last
    )
    layer_out, *grads = pl.pallas_call(
        layer_kernel,
        out_shape=(
            jax.ShapeDtypeStruct((rows, width), BF16),
            *(jax.ShapeDtypeStruct(grad.shape, grad.dtype) for grad in grads),
        ),
        in_specs=[hbm] * 6,
        out_specs=(hbm,) * 5,
        scratch_shapes=[
            vmem((rows, hd), BF16),
            vmem((n_zy, CORES, 16, width), BF16),
            vmem((rows, width), BF16),
            *(vmem(grad.shape, grad.dtype) for grad in grads),
            dma((LAYER_PARTS + 1,)), dma((LAYER_PARTS,)), dma((4,)), dma((4,)),
        ],
        compiler_params=pltpu.CompilerParams(vmem_limit_bytes=60 * 1024 * 1024),
    )(attn, weight, *grads)
    weight_grad = grads.pop()
    return (layer_out[None], *(grad[None] for grad in grads), weight_grad)


def solution(mesh, n_y=Y_CHIPS):
    return jax.shard_map(
        functools.partial(body, mesh.shape["seq"], mesh.shape["dp"], n_y),
        mesh=mesh,
        in_specs=(
            P("dp", "seq", None),
            P("dp", "seq", None),
            P("dp", "seq", None),
            P("seq", None),
            P("dp", "seq", None),
            P("dp", "seq"),
            P("dp", "seq"),
        ),
        out_specs=(
            P("dp", "seq", None),
            P("dp", "seq", None),
            P("dp", "seq", None),
            P("dp", "seq", None),
            P("seq", None),
        ),
        check_vma=False,
    )
```

```python
import functools
import math

import jax
import jax.numpy as jnp
from jax import lax
from jax.experimental import pallas as pl
from jax.experimental.pallas import tpu as pltpu
from jax.sharding import PartitionSpec as P

HDIM = 128
BLOCK = 128
HALF = 256
CORES = 2
Y_CHIPS = 4
F32 = jnp.float32
BF16 = jnp.bfloat16
NEVER = -1e30
LAYER_PARTS = 4
PLAN = (
    "hs1 ag0 f00 hs2", "f01 f10 wg0 hs3", "ag1 f11 f02 wg1", "xs0 f03 ag2 f12",
    "wg2 xs1 zs4 f13", "wg3 xs2 ag3 ga0", "zs3 b10 xs3 b00", "zs2 ag4 ga1 b11",
    "b01 zs1 ga2 b12", "b02 ag5 zs0 ys0", "ga3 kp0 b13 yx0", "b03 xx0 gs0 gs1",
)
SMALL_PLAN = (
    "ag0 hs1 f00 f10", "wg0 ag1 f01 xs0", "ag2 f11 wg1 ga0", "zs2 xs1 b10 b00",
    "zs1 ag3 ga1 kp0", "b11 zs0 ys0 b01", "yx0 gs0 gs1 xx0",
)


def dot(a, b, dims):
    return lax.dot_general(a, b, (dims, ((), ())), preferred_element_type=F32)


def kernel(
    sizes,
    q_hbm, k_hbm, v_hbm, shard_hbm, go_hbm, first_ref, last_ref,
    attn_hbm, w_hbm, dq_hbm, dk_hbm, dv_hbm, wgrad_hbm,
    w, q, kg, vg, go, probs, attn_t, attn, ga, bias,
    dq, dk_own, dv_own, dk_send, dv_send, dk_recv, dv_recv,
    wg, sib_recv, side_send, side_recv, plus_send, plus_recv, minus_send, minus_recv,
    z_sum, y_send, y_recv, x_all, wgrad,
    load_sem, store_sem,
    halo_send_sem, halo_recv_sem,
    agy_send_sem, agy_recv_sem, agp_send_sem, agp_recv_sem, agm_send_sem, agm_recv_sem,
    agx_send_sem, agx_recv_sem, ags_send_sem, ags_recv_sem,
    rsw_send_sem, rsw_recv_sem,
    rss_send_sem, rss_recv_sem, rsp_send_sem, rsp_recv_sem, rsm_send_sem, rsm_recv_sem,
    rsy_send_sem, rsy_recv_sem, rsx_send_sem, rsx_recv_sem,
    grad_send_sem, grad_recv_sem,
):
    n_seq, n_x, n_y, n_z, n_plus, n_minus, heads, width, norm = sizes
    scale = 1.0 / math.sqrt(HDIM)
    s = lax.axis_index("seq")
    x = lax.axis_index("dp")
    c = s % CORES
    zy = s // CORES
    y = zy % n_y
    z = zy // n_y

    def at_zy(z_index, y_index, core):
        return (z_index * n_y + y_index) * CORES + core

    sibling = s + 1 - 2 * c
    across = (s + 2 * c - 1 + n_seq) % n_seq
    z_next = at_zy((z + 1) % n_z, y, c)
    z_prev = at_zy((z + n_z - 1) % n_z, y, c)
    y_peers = [at_zy(z, (y + j) % n_y, c) for j in range(1, n_y)]
    x_peers = [(x + j) % n_x for j in range(1, n_x)]
    x_next, x_prev = (x + 1) % n_x, (x + n_x - 1) % n_x
    half, quarter = width // 2, width // 4
    mine, other = (x % 2) * half, (1 - x % 2) * half

    def wide(start, size):
        return pl.ds(pl.multiple_of(start, 128), size)

    pairs = n_z // 2

    def near_first(z_index):
        side = 2 * (z_index % 2) - 1
        steps = (0, side, -side, 2)[:pairs]
        return [(z_index // 2 + step + pairs) % pairs for step in steps]

    near, far = near_first(z), near_first(z)[::-1]

    partners = (sibling, across)
    group = (1 - c, c)

    loads = []

    def load(src, dst):
        copy = pltpu.make_async_copy(src, dst, load_sem.at[len(loads)])
        copy.start()
        loads.append(copy)
        return copy

    def token_rows(t):
        return pl.ds(pl.multiple_of(group[t] * HALF, HALF), HALF)

    load_shard = load(shard_hbm, w.at[zy, c])
    load_q, load_k, load_v, load_go = [], [], [], []
    for t in range(2):
        load_q.append(load(q_hbm.at[token_rows(t)], q.at[t]))
        load_k.append(load(k_hbm.at[token_rows(t)], kg.at[t, pl.ds(0, HALF)]))
        load_v.append(load(v_hbm.at[token_rows(t)], vg.at[t, pl.ds(0, HALF)]))
    for t in range(2):
        load_go.append(load(go_hbm.at[token_rows(t)], go.at[t]))

    barrier = pltpu.get_barrier_semaphore()
    seq_peers = [sibling, across, z_next, z_prev] + y_peers
    for peer in seq_peers:
        pl.semaphore_signal(
            barrier, inc=1, device_id={"seq": peer}, device_id_type=pl.DeviceIdType.MESH
        )
    for peer in x_peers:
        pl.semaphore_signal(
            barrier, inc=1, device_id={"dp": peer}, device_id_type=pl.DeviceIdType.MESH
        )
    pl.semaphore_wait(barrier, len(seq_peers) + len(x_peers))

    sent = []

    def send(src, dst, send_sem, recv_sem, target):
        copy = pltpu.make_async_remote_copy(
            src_ref=src,
            dst_ref=dst,
            send_sem=send_sem,
            recv_sem=recv_sem,
            device_id=target,
            device_id_type=pl.DeviceIdType.MESH,
        )
        copy.start()
        sent.append(copy)
        return copy

    agy = [
        send(
            shard_hbm, w.at[zy, c], agy_send_sem.at[j], agy_recv_sem.at[j], {"seq": peer}
        )
        for j, peer in enumerate(y_peers)
    ]

    def pair_cols(r):
        return pl.ds(pl.multiple_of(r * HALF, HALF), HALF)

    halo = {}

    def share_keys(t, i):
        r = near_first(partners[t] // CORES // n_y)[::-1][i]
        halo[t, i] = []
        for which, (src, dst) in enumerate(((k_hbm, kg), (v_hbm, vg))):
            n = (t * pairs + i) * 2 + which
            halo[t, i].append(
                send(
                    src.at[token_rows(t), pair_cols(r)],
                    dst.at[t, pl.ds(HALF, HALF), pair_cols(r)],
                    halo_send_sem.at[n],
                    halo_recv_sem.at[n],
                    {"seq": partners[t]},
                )
            )

    share_keys(1, 0)
    for i in range(pairs):
        share_keys(0, i)

    def slab(z_index, start, size):
        return w.at[pl.ds(z_index * n_y, n_y), c, :, wide(start, size)]

    ag_sib, ag_side = {}, {}

    def share_slab(key, z_index, start, size):
        i = len(ag_sib)
        piece = slab(z_index, start, size)
        ag_sib[key] = send(
            piece, piece, ags_send_sem.at[i], ags_recv_sem.at[i], {"seq": sibling}
        )

    def pass_aside(z_index, key):
        ag_side[key] = []
        for start, peer in ((mine, x_next), (mine + quarter, x_prev)):
            i = 2 * len(ag_side) - 2 + len(ag_side[key])
            piece = slab(z_index, start, quarter)
            ag_side[key].append(
                send(piece, piece, agx_send_sem.at[i], agx_recv_sem.at[i], {"dp": peer})
            )

    agp, agm = [], []

    def ag_step(k):
        if k == 0:
            load_shard.wait()
            for copy in agy:
                copy.wait_recv()
        from_prev, from_next = (z + n_z - k) % n_z, (z + k) % n_z
        if 0 < k <= n_plus:
            agp[k - 1].wait_recv()
        if k < n_plus:
            piece = slab(from_prev, mine, half)
            agp.append(
                send(piece, piece, agp_send_sem.at[k], agp_recv_sem.at[k], {"seq": z_next})
            )
        if 0 < k <= n_plus:
            pass_aside(from_prev, (1, k))
        if 0 < k <= n_minus:
            agm[k - 1].wait_recv()
        if k < n_minus:
            piece = slab(from_next, mine, half)
            agm.append(
                send(piece, piece, agm_send_sem.at[k], agm_recv_sem.at[k], {"seq": z_prev})
            )
        if 0 < k <= n_minus:
            pass_aside(from_next, (-1, k))
        if k == 0:
            share_slab((0, 0), z, 0, width)
        if 0 < k <= n_plus:
            share_slab((1, k), from_prev, mine, half)
        if 0 < k <= n_minus:
            share_slab((-1, k), from_next, mine, half)
        for way, last in ((1, n_plus), (-1, n_minus)):
            if 1 <= k - 1 <= last:
                for copy in ag_side[way, k - 1]:
                    copy.wait_recv()
                share_slab((way, k - 1, 1), (z + n_z - way * (k - 1)) % n_z, other, half)

    for t in range(2):
        key_row = lax.broadcasted_iota(jnp.int32, (2 * HALF, HALF), 0)
        query_col = lax.broadcasted_iota(jnp.int32, (2 * HALF, HALF), 1)
        own_base = s * 4 + 2 * group[t]
        halo_base = s * 4 - 2 + 6 * group[t]
        key_block = jnp.where(
            key_row < HALF,
            own_base + (key_row >> 7),
            halo_base - 2 + (key_row >> 7),
        )
        early = query_col < BLOCK
        lower = jnp.where(early, first_ref[0, 2 * group[t]], first_ref[0, 2 * group[t] + 1])
        upper = jnp.where(early, last_ref[0, 2 * group[t]], last_ref[0, 2 * group[t] + 1])
        inside = (key_block >= lower) & (key_block < upper)
        bias[t] = jnp.where(inside, 0.0, NEVER)

    def forward(t, i):
        if i == 0:
            load_q[t].wait()
            load_k[t].wait()
            load_v[t].wait()
        for copy in halo[t, i]:
            copy.wait_recv()
        for h in (2 * far[i], 2 * far[i] + 1):
            cols = wide(h * HDIM, HDIM)
            scores = dot(kg[t, :, cols], q[t, :, cols], ((1,), (1,))) * scale + bias[t]
            highest = jnp.max(scores, axis=0, keepdims=True)
            raised = jnp.exp(scores - highest)
            total = jnp.sum(raised, axis=0, keepdims=True)
            p = raised * (1.0 / total)
            probs[t, h] = p
            out_t = dot(vg[t, :, cols], p.astype(BF16), ((0,), (0,)))
            attn_t[cols, pl.ds(t * HALF, HALF)] = out_t.astype(BF16)
            attn[pl.ds(t * HALF, HALF), cols] = out_t.T.astype(BF16)

    grads = []

    def backward(t, i):
        for h in (2 * near[i], 2 * near[i] + 1):
            cols = wide(h * HDIM, HDIM)
            p = probs[t, h]
            grad_rows = ga[pl.ds(t * HALF, HALF), cols]
            grad_p = dot(vg[t, :, cols], grad_rows, ((1,), (1,)))
            row_term = jnp.sum(p * grad_p, axis=0, keepdims=True)
            grad_s = (p * (grad_p - row_term) * scale).astype(BF16)
            dq_t = dot(kg[t, :, cols], grad_s, ((0,), (0,)))
            dq[t, :, cols] = dq_t.T.astype(BF16)
            dk = dot(grad_s, q[t, :, cols], ((1,), (0,)))
            dv = dot(p.astype(BF16), grad_rows, ((1,), (0,)))
            dk_own[t, :, cols] = dk[:HALF]
            dv_own[t, :, cols] = dv[:HALF]
            dk_send[t, :, cols] = dk[HALF:].astype(BF16)
            dv_send[t, :, cols] = dv[HALF:].astype(BF16)
        for which, (src, dst) in enumerate(((dk_send, dk_recv), (dv_send, dv_recv))):
            n = (t * pairs + i) * 2 + which
            piece = pair_cols(near[i])
            copy = send(
                src.at[t, :, piece], dst.at[t, :, piece], grad_send_sem.at[n],
                grad_recv_sem.at[n], {"seq": partners[t]},
            )
            grads.append((copy, t))

    hd = heads * HDIM
    col_width = min(512, width)

    def weight_rows(i):
        r = far[i]
        if i == 0:
            for copy in load_go:
                copy.wait()
        left = attn_t[pair_cols(r), :]

        def tile(n, carry):
            cols = wide(n * col_width, col_width)
            right = go[:, :, cols].reshape(2 * HALF, col_width)
            block = dot(left, right, ((1,), (0,))).astype(BF16)
            wg[pl.ds(r * 8, 8), :, :, cols] = block.reshape(8, CORES, 16, col_width)
            return carry

        lax.fori_loop(0, width // col_width, tile, 0)
        rss.append(
            send(
                wg.at[pl.ds(r * 8, 8), 1 - c], sib_recv.at[pl.ds(r * 8, 8)], rss_send_sem.at[i],
                rss_recv_sem.at[i], {"seq": sibling},
            )
        )

    def grad_attn(i):
        for k in range(i + 2):
            for way in (1, -1):
                for key in ((way, k), (way, k, 1)):
                    if key in ag_sib and key not in ag_here:
                        ag_sib[key].wait_recv()
                        ag_here.append(key)
        if i == 0:
            ag_sib[0, 0].wait_recv()
        rows = w[pl.ds(near[i] * 8, 8)].reshape(HALF, width)
        tile = dot(go[...].reshape(2 * HALF, width), rows, ((1,), (1,)))
        ga[:, pair_cols(near[i])] = tile.astype(BF16)

    rss, ag_here = [], []

    rsw = {}

    def aside(way, k):
        i = len(rsw)
        first_row = (z + way * k + n_z) % n_z * n_y

        def add_cores(j, carry):
            for part in range(2):
                cols = wide(other + part * quarter, quarter)
                total = wg[first_row + j, c, :, cols].astype(F32)
                total = total + sib_recv[first_row + j, :, cols].astype(F32)
                side_send[i, part, j] = total.astype(BF16)
            return carry

        lax.fori_loop(0, n_y, add_cores, 0)
        rsw[way, k] = i, [
            send(
                side_send.at[i, part], side_recv.at[i, part], rsw_send_sem.at[2 * i + part],
                rsw_recv_sem.at[2 * i + part], {"dp": peer},
            )
            for part, peer in enumerate((x_next, x_prev))
        ]

    def aside_level(level):
        rss[level].wait_recv()
        k = n_plus - level
        aside(1, k)
        if k <= n_minus:
            aside(-1, k)
        if k == 1:
            aside(1, 0)

    rsp, rsm = {}, {}

    def chain(way, k):
        i, copies = rsw[way, k]
        first_row = (z + way * k + n_z) % n_z * n_y
        for copy in copies:
            copy.wait_recv()
        arrivals = []
        if (way == 1 or k == 0) and k < n_plus:
            rsp[k + 1].wait_recv()
            arrivals.append(plus_recv)
        if (way == -1 or k == 0) and k < n_minus:
            rsm[k + 1].wait_recv()
            arrivals.append(minus_recv)

        def add(j, carry):
            for part in range(2):
                cols = wide(mine + part * quarter, quarter)
                here = pl.ds(part * quarter, quarter)
                total = wg[first_row + j, c, :, cols].astype(F32)
                total = total + sib_recv[first_row + j, :, cols].astype(F32)
                total = total + side_recv[i, part, j].astype(F32)
                for ref in arrivals:
                    total = total + ref[k, j, :, here].astype(F32)
                if k == 0:
                    z_sum[j, :, here] = total
                    y_send[j, :, here] = total.astype(BF16)
                elif way == 1:
                    plus_send[k - 1, j, :, here] = total.astype(BF16)
                else:
                    minus_send[k - 1, j, :, here] = total.astype(BF16)
            return carry

        lax.fori_loop(0, n_y, add, 0)
        if k and way == 1:
            rsp[k] = send(
                plus_send.at[k - 1], plus_recv.at[k - 1], rsp_send_sem.at[k - 1],
                rsp_recv_sem.at[k - 1], {"seq": z_next},
            )
        if k and way == -1:
            rsm[k] = send(
                minus_send.at[k - 1], minus_recv.at[k - 1], rsm_send_sem.at[k - 1],
                rsm_recv_sem.at[k - 1], {"seq": z_prev},
            )

    def chain_level(k):
        if k <= n_plus:
            chain(1, k)
        if 0 < k <= n_minus:
            chain(-1, k)

    stores = []

    def store(src, dst):
        copy = pltpu.make_async_copy(src, dst, store_sem.at[len(stores)])
        copy.start()
        stores.append(copy)

    rsy, rsx = [], []

    def along_y(_):
        for j, peer in enumerate(y_peers, 1):
            rsy.append(
                send(
                    y_send.at[(y + j) % n_y], y_recv.at[j - 1], rsy_send_sem.at[j - 1],
                    rsy_recv_sem.at[j - 1], {"seq": peer},
                )
            )

    def along_x(_):
        total = z_sum[y]
        for j, copy in enumerate(rsy):
            copy.wait_recv()
            total = total + y_recv[j].astype(F32)
        x_all[x] = total.astype(BF16)
        for j, peer in enumerate(x_peers):
            rsx.append(
                send(
                    x_all.at[x], x_all.at[x], rsx_send_sem.at[j], rsx_recv_sem.at[j],
                    {"dp": peer},
                )
            )

    def last_sum(_):
        for copy in rsx:
            copy.wait_recv()
        for parity in range(2):
            total = x_all[parity].astype(F32)
            for j in range(parity + 2, n_x, 2):
                total = total + x_all[j].astype(F32)
            wgrad[:, pl.ds(parity * half, half)] = total * (1.0 / norm)
        store(wgrad, wgrad_hbm)

    def keep(_):
        for t in range(2):
            store(attn.at[pl.ds(t * HALF, HALF)], attn_hbm.at[token_rows(t)])
        store(w, w_hbm)

    def grad_sum(t):
        store(dq.at[t], dq_hbm.at[token_rows(t)])
        for copy, slot in grads:
            if slot == t:
                copy.wait()
        for own, got, out, hbm in (
            (dk_own, dk_recv, dk_send, dk_hbm), (dv_own, dv_recv, dv_send, dv_hbm)
        ):
            def add_rows(i, carry, own=own, got=got, out=out):
                rows = pl.ds(pl.multiple_of(i * 32, 32), 32)
                out[t, rows] = (own[t, rows] + got[t, rows].astype(F32)).astype(BF16)
                return carry

            lax.fori_loop(0, HALF // 32, add_rows, 0)
            store(out.at[t], hbm.at[token_rows(t)])

    plan = PLAN if n_z == 8 else SMALL_PLAN
    steps = {
        "hs": functools.partial(share_keys, 1),
        "ag": ag_step, "f0": functools.partial(forward, 0), "f1": functools.partial(forward, 1),
        "wg": weight_rows, "xs": aside_level, "zs": chain_level, "ga": grad_attn,
        "b0": functools.partial(backward, 0), "b1": functools.partial(backward, 1),
        "ys": along_y, "yx": along_x, "xx": last_sum, "kp": keep, "gs": grad_sum,
    }
    for item in " ".join(plan).split():
        steps[item[:2]](int(item[2:]))

    waited = [copy for copy, _ in grads]
    for copy in sent:
        if not any(copy is other for other in waited):
            copy.wait_send()
    for copy in stores:
        copy.wait()


def layer_kernel(
    attn_hbm, w_hbm, dq_in, dk_in, dv_in, wgrad_in,
    layer_hbm, dq_out, dk_out, dv_out, wgrad_out,
    attn, w, layer, dq, dk, dv, wgrad,
    load_sem, store_sem, in_sem, out_sem,
):
    hd, width = attn.shape[1], layer.shape[1]
    size = width // LAYER_PARTS
    parts = [pl.ds(n * size, size) for n in range(LAYER_PARTS)]
    loads = [pltpu.make_async_copy(attn_hbm, attn, load_sem.at[LAYER_PARTS])]
    for n, cols in enumerate(parts):
        loads.append(
            pltpu.make_async_copy(
                w_hbm.at[:, :, :, cols], w.at[:, :, :, cols], load_sem.at[n]
            )
        )
    moved = (
        (dq_in, dq, dq_out), (dk_in, dk, dk_out), (dv_in, dv, dv_out), (wgrad_in, wgrad, wgrad_out)
    )
    moves = [
        pltpu.make_async_copy(source, held, in_sem.at[n])
        for n, (source, held, _) in enumerate(moved)
    ]
    for copy in loads + moves:
        copy.start()
    stores = []
    loads[0].wait()
    for n, cols in enumerate(parts):
        loads[n + 1].wait()
        right = w[:, :, :, cols].reshape(hd, size)
        layer[:, cols] = dot(attn[...], right, ((1,), (0,))).astype(BF16)
        stores.append(
            pltpu.make_async_copy(layer.at[:, cols], layer_hbm.at[:, cols], store_sem.at[n])
        )
        stores[-1].start()
        if n < len(moved):
            _, held, target = moved[n]
            moves[n].wait()
            stores.append(pltpu.make_async_copy(held, target, out_sem.at[n]))
            stores[-1].start()
    for copy in stores:
        copy.wait()


def body(n_seq, n_x, n_y, queries, memory_keys, memory_values, out_weight, grad_out, key_first, key_last):
    rows, hd = queries.shape[1:]
    width = grad_out.shape[2]
    heads = hd // HDIM
    n_z = n_seq // (CORES * n_y)
    n_plus = n_z // 2
    n_minus = n_z - 1 - n_plus
    n_zy = n_z * n_y
    norm = math.sqrt(n_seq * rows)
    sizes = (n_seq, n_x, n_y, n_z, n_plus, n_minus, heads, width, norm)
    vmem, dma = pltpu.VMEM, pltpu.SemaphoreType.DMA
    scratch = [
        vmem((n_zy, CORES, 16, width), BF16),
        vmem((2, HALF, hd), BF16),
        vmem((2, 2 * HALF, hd), BF16),
        vmem((2, 2 * HALF, hd), BF16),
        vmem((2, HALF, width), BF16),
        vmem((2, heads, 2 * HALF, HALF), F32),
        vmem((hd, 2 * HALF), BF16),
        vmem((2 * HALF, hd), BF16),
        vmem((2 * HALF, hd), BF16),
        vmem((2, 2 * HALF, HALF), F32),
        vmem((2, HALF, hd), BF16),
        vmem((2, HALF, hd), F32),
        vmem((2, HALF, hd), F32),
        vmem((2, HALF, hd), BF16),
        vmem((2, HALF, hd), BF16),
        vmem((2, HALF, hd), BF16),
        vmem((2, HALF, hd), BF16),
        vmem((n_zy, CORES, 16, width), BF16),
        vmem((n_zy, 16, width), BF16),
        vmem((n_z, 2, n_y, 16, width // 4), BF16),
        vmem((n_z, 2, n_y, 16, width // 4), BF16),
        vmem((n_plus, n_y, 16, width // 2), BF16),
        vmem((n_plus, n_y, 16, width // 2), BF16),
        vmem((max(n_minus, 1), n_y, 16, width // 2), BF16),
        vmem((max(n_minus, 1), n_y, 16, width // 2), BF16),
        vmem((n_y, 16, width // 2), F32),
        vmem((n_y, 16, width // 2), BF16),
        vmem((n_y - 1, 16, width // 2), BF16),
        vmem((n_x, 16, width // 2), BF16),
        vmem((16, width), F32),
        dma((9,)),
        dma((10,)),
        dma((2 * n_z,)), dma((2 * n_z,)),
        dma((n_y - 1,)), dma((n_y - 1,)),
        dma((n_plus,)), dma((n_plus,)),
        dma((max(n_minus, 1),)), dma((max(n_minus, 1),)),
        dma((2 * n_z,)), dma((2 * n_z,)),
        dma((2 * n_z,)), dma((2 * n_z,)),
        dma((2 * n_z,)), dma((2 * n_z,)),
        dma((hd // HALF,)), dma((hd // HALF,)),
        dma((n_plus,)), dma((n_plus,)),
        dma((max(n_minus, 1),)), dma((max(n_minus, 1),)),
        dma((n_y - 1,)), dma((n_y - 1,)),
        dma((n_x - 1,)), dma((n_x - 1,)),
        dma((2 * n_z,)), dma((2 * n_z,)),
    ]
    hbm = pl.BlockSpec(memory_space=pl.ANY)
    smem = pl.BlockSpec(memory_space=pltpu.SMEM)
    attn, weight, *grads = pl.pallas_call(
        functools.partial(kernel, sizes),
        out_shape=(
            jax.ShapeDtypeStruct((rows, hd), BF16),
            jax.ShapeDtypeStruct((n_zy, CORES, 16, width), BF16),
            jax.ShapeDtypeStruct((rows, hd), BF16),
            jax.ShapeDtypeStruct((rows, hd), BF16),
            jax.ShapeDtypeStruct((rows, hd), BF16),
            jax.ShapeDtypeStruct((16, width), F32),
        ),
        in_specs=[hbm] * 5 + [smem] * 2,
        out_specs=(hbm,) * 6,
        scratch_shapes=scratch,
        compiler_params=pltpu.CompilerParams(
            collective_id=0, has_side_effects=True, vmem_limit_bytes=60 * 1024 * 1024
        ),
    )(
        queries[0], memory_keys[0], memory_values[0], out_weight, grad_out[0], key_first, key_last
    )
    layer_out, *grads = pl.pallas_call(
        layer_kernel,
        out_shape=(
            jax.ShapeDtypeStruct((rows, width), BF16),
            *(jax.ShapeDtypeStruct(grad.shape, grad.dtype) for grad in grads),
        ),
        in_specs=[hbm] * 6,
        out_specs=(hbm,) * 5,
        scratch_shapes=[
            vmem((rows, hd), BF16),
            vmem((n_zy, CORES, 16, width), BF16),
            vmem((rows, width), BF16),
            *(vmem(grad.shape, grad.dtype) for grad in grads),
            dma((LAYER_PARTS + 1,)), dma((LAYER_PARTS,)), dma((4,)), dma((4,)),
        ],
        compiler_params=pltpu.CompilerParams(vmem_limit_bytes=60 * 1024 * 1024),
    )(attn, weight, *grads)
    weight_grad = grads.pop()
    return (layer_out[None], *(grad[None] for grad in grads), weight_grad)


def solution(mesh, n_y=Y_CHIPS):
    return jax.shard_map(
        functools.partial(body, mesh.shape["seq"], mesh.shape["dp"], n_y),
        mesh=mesh,
        in_specs=(
            P("dp", "seq", None),
            P("dp", "seq", None),
            P("dp", "seq", None),
            P("seq", None),
            P("dp", "seq", None),
            P("dp", "seq"),
            P("dp", "seq"),
        ),
        out_specs=(
            P("dp", "seq", None),
            P("dp", "seq", None),
            P("dp", "seq", None),
            P("dp", "seq", None),
            P("seq", None),
        ),
        check_vma=False,
    )
```

```python
import functools
import math

import jax
import jax.numpy as jnp
from jax import lax
from jax.experimental import pallas as pl
from jax.experimental.pallas import tpu as pltpu
from jax.sharding import PartitionSpec as P

HDIM = 128
BLOCK = 128
HALF = 256
CORES = 2
Y_CHIPS = 4
F32 = jnp.float32
BF16 = jnp.bfloat16
NEVER = -1e30
LAYER_PARTS = 4
PLAN = (
    "hs1 ag0 f00 hs2", "f01 f10 wg0 hs3", "ag1 f11 wg1 f02", "xs0 f03 ag2 f12",
    "wg2 xs1 zs4 f13", "wg3 xs2 ag3 zs3", "xs3 ga0 b10 b00", "zs2 ag4 ga1 b11",
    "b01 zs1 ga2 b12", "ag5 b02 zs0 ys0", "ga3 kp0 b13 b03", "yx0 gs0 xx0 gs1",
)
SMALL_PLAN = (
    "ag0 hs1 f00 f10", "wg0 ag1 f01 xs0", "ag2 f11 wg1 ga0", "zs2 xs1 b10 b00",
    "zs1 ag3 ga1 kp0", "b11 zs0 ys0 b01", "yx0 gs0 gs1 xx0",
)


def dot(a, b, dims):
    return lax.dot_general(a, b, (dims, ((), ())), preferred_element_type=F32)


def kernel(
    sizes,
    q_hbm, k_hbm, v_hbm, shard_hbm, go_hbm, first_ref, last_ref,
    attn_hbm, w_hbm, dq_hbm, dk_hbm, dv_hbm, wgrad_hbm,
    w, q, kg, vg, go, probs, attn_t, attn, ga, bias,
    dq, dk_own, dv_own, dk_send, dv_send, dk_recv, dv_recv,
    wg, sib_recv, side_send, side_recv, plus_send, plus_recv, minus_send, minus_recv,
    z_sum, y_send, y_recv, x_all, wgrad,
    load_sem, store_sem,
    halo_send_sem, halo_recv_sem,
    agy_send_sem, agy_recv_sem, agp_send_sem, agp_recv_sem, agm_send_sem, agm_recv_sem,
    agx_send_sem, agx_recv_sem, ags_send_sem, ags_recv_sem,
    rsw_send_sem, rsw_recv_sem,
    rss_send_sem, rss_recv_sem, rsp_send_sem, rsp_recv_sem, rsm_send_sem, rsm_recv_sem,
    rsy_send_sem, rsy_recv_sem, rsx_send_sem, rsx_recv_sem,
    grad_send_sem, grad_recv_sem,
):
    n_seq, n_x, n_y, n_z, n_plus, n_minus, heads, width, norm = sizes
    scale = 1.0 / math.sqrt(HDIM)
    log_scale = scale * math.log2(math.e)
    s = lax.axis_index("seq")
    x = lax.axis_index("dp")
    c = s % CORES
    zy = s // CORES
    y = zy % n_y
    z = zy // n_y

    def at_zy(z_index, y_index, core):
        return (z_index * n_y + y_index) * CORES + core

    sibling = s + 1 - 2 * c
    across = (s + 2 * c - 1 + n_seq) % n_seq
    z_next = at_zy((z + 1) % n_z, y, c)
    z_prev = at_zy((z + n_z - 1) % n_z, y, c)
    y_peers = [at_zy(z, (y + j) % n_y, c) for j in range(1, n_y)]
    x_peers = [(x + j) % n_x for j in range(1, n_x)]
    x_next, x_prev = (x + 1) % n_x, (x + n_x - 1) % n_x
    half, quarter = width // 2, width // 4
    mine, other = (x % 2) * half, (1 - x % 2) * half

    def wide(start, size):
        return pl.ds(pl.multiple_of(start, 128), size)

    pairs = n_z // 2

    def near_first(z_index):
        side = 2 * (z_index % 2) - 1
        steps = (0, side, -side, 2)[:pairs]
        return [(z_index // 2 + step + pairs) % pairs for step in steps]

    near, far = near_first(z), near_first(z)[::-1]

    partners = (sibling, across)
    group = (1 - c, c)

    loads = []

    def load(src, dst):
        copy = pltpu.make_async_copy(src, dst, load_sem.at[len(loads)])
        copy.start()
        loads.append(copy)
        return copy

    def token_rows(t):
        return pl.ds(pl.multiple_of(group[t] * HALF, HALF), HALF)

    load_shard = load(shard_hbm, w.at[zy, c])
    load_q, load_k, load_v, load_go = [], [], [], []
    for t in range(2):
        load_q.append(load(q_hbm.at[token_rows(t)], q.at[t]))
        load_k.append(load(k_hbm.at[token_rows(t)], kg.at[t, pl.ds(0, HALF)]))
        load_v.append(load(v_hbm.at[token_rows(t)], vg.at[t, pl.ds(0, HALF)]))
    for t in range(2):
        load_go.append(load(go_hbm.at[token_rows(t)], go.at[t]))

    barrier = pltpu.get_barrier_semaphore()
    seq_peers = [sibling, across, z_next, z_prev] + y_peers
    for peer in seq_peers:
        pl.semaphore_signal(
            barrier, inc=1, device_id={"seq": peer}, device_id_type=pl.DeviceIdType.MESH
        )
    for peer in x_peers:
        pl.semaphore_signal(
            barrier, inc=1, device_id={"dp": peer}, device_id_type=pl.DeviceIdType.MESH
        )
    pl.semaphore_wait(barrier, len(seq_peers) + len(x_peers))

    sent = []

    def send(src, dst, send_sem, recv_sem, target):
        copy = pltpu.make_async_remote_copy(
            src_ref=src,
            dst_ref=dst,
            send_sem=send_sem,
            recv_sem=recv_sem,
            device_id=target,
            device_id_type=pl.DeviceIdType.MESH,
        )
        copy.start()
        sent.append(copy)
        return copy

    agy = [
        send(
            shard_hbm, w.at[zy, c], agy_send_sem.at[j], agy_recv_sem.at[j], {"seq": peer}
        )
        for j, peer in enumerate(y_peers)
    ]

    def pair_cols(r):
        return pl.ds(pl.multiple_of(r * HALF, HALF), HALF)

    halo = {}

    def share_keys(t, i):
        r = near_first(partners[t] // CORES // n_y)[::-1][i]
        halo[t, i] = []
        for which, (src, dst) in enumerate(((k_hbm, kg), (v_hbm, vg))):
            n = (t * pairs + i) * 2 + which
            halo[t, i].append(
                send(
                    src.at[token_rows(t), pair_cols(r)],
                    dst.at[t, pl.ds(HALF, HALF), pair_cols(r)],
                    halo_send_sem.at[n],
                    halo_recv_sem.at[n],
                    {"seq": partners[t]},
                )
            )

    share_keys(1, 0)
    for i in range(pairs):
        share_keys(0, i)

    def slab(z_index, start, size):
        return w.at[pl.ds(z_index * n_y, n_y), c, :, wide(start, size)]

    ag_sib, ag_side = {}, {}

    def share_slab(key, z_index, start, size):
        i = len(ag_sib)
        piece = slab(z_index, start, size)
        ag_sib[key] = send(
            piece, piece, ags_send_sem.at[i], ags_recv_sem.at[i], {"seq": sibling}
        )

    def pass_aside(z_index, key):
        ag_side[key] = []
        for start, peer in ((mine, x_next), (mine + quarter, x_prev)):
            i = 2 * len(ag_side) - 2 + len(ag_side[key])
            piece = slab(z_index, start, quarter)
            ag_side[key].append(
                send(piece, piece, agx_send_sem.at[i], agx_recv_sem.at[i], {"dp": peer})
            )

    agp, agm = [], []

    def ag_step(k):
        if k == 0:
            load_shard.wait()
            for copy in agy:
                copy.wait_recv()
        from_prev, from_next = (z + n_z - k) % n_z, (z + k) % n_z
        if 0 < k <= n_plus:
            agp[k - 1].wait_recv()
        if k < n_plus:
            piece = slab(from_prev, mine, half)
            agp.append(
                send(piece, piece, agp_send_sem.at[k], agp_recv_sem.at[k], {"seq": z_next})
            )
        if 0 < k <= n_plus:
            pass_aside(from_prev, (1, k))
        if 0 < k <= n_minus:
            agm[k - 1].wait_recv()
        if k < n_minus:
            piece = slab(from_next, mine, half)
            agm.append(
                send(piece, piece, agm_send_sem.at[k], agm_recv_sem.at[k], {"seq": z_prev})
            )
        if 0 < k <= n_minus:
            pass_aside(from_next, (-1, k))
        if k == 0:
            share_slab((0, 0), z, 0, width)
        if 0 < k <= n_plus:
            share_slab((1, k), from_prev, mine, half)
        if 0 < k <= n_minus:
            share_slab((-1, k), from_next, mine, half)
        for way, last in ((1, n_plus), (-1, n_minus)):
            if 1 <= k - 1 <= last:
                for copy in ag_side[way, k - 1]:
                    copy.wait_recv()
                share_slab((way, k - 1, 1), (z + n_z - way * (k - 1)) % n_z, other, half)

    for t in range(2):
        key_row = lax.broadcasted_iota(jnp.int32, (2 * HALF, HALF), 0)
        query_col = lax.broadcasted_iota(jnp.int32, (2 * HALF, HALF), 1)
        own_base = s * 4 + 2 * group[t]
        halo_base = s * 4 - 2 + 6 * group[t]
        key_block = jnp.where(
            key_row < HALF,
            own_base + (key_row >> 7),
            halo_base - 2 + (key_row >> 7),
        )
        early = query_col < BLOCK
        lower = jnp.where(early, first_ref[0, 2 * group[t]], first_ref[0, 2 * group[t] + 1])
        upper = jnp.where(early, last_ref[0, 2 * group[t]], last_ref[0, 2 * group[t] + 1])
        inside = (key_block >= lower) & (key_block < upper)
        bias[t] = jnp.where(inside, 0.0, NEVER)

    def forward(t, i):
        if i == 0:
            load_q[t].wait()
            load_k[t].wait()
            load_v[t].wait()
        for copy in halo[t, i]:
            copy.wait_recv()
        for h in (2 * far[i], 2 * far[i] + 1):
            cols = wide(h * HDIM, HDIM)
            scores = dot(kg[t, :, cols], q[t, :, cols], ((1,), (1,))) * log_scale + bias[t]
            highest = jnp.max(scores, axis=0, keepdims=True)
            raised = jnp.exp2(scores - highest)
            total = jnp.sum(raised, axis=0, keepdims=True)
            p = raised * (1.0 / total)
            probs[t, h] = p
            out_t = dot(vg[t, :, cols], p.astype(BF16), ((0,), (0,)))
            attn_t[cols, pl.ds(t * HALF, HALF)] = out_t.astype(BF16)
            attn[pl.ds(t * HALF, HALF), cols] = out_t.T.astype(BF16)

    grads = []

    def backward(t, i):
        for h in (2 * near[i], 2 * near[i] + 1):
            cols = wide(h * HDIM, HDIM)
            p = probs[t, h]
            grad_rows = ga[pl.ds(t * HALF, HALF), cols]
            grad_p = dot(vg[t, :, cols], grad_rows, ((1,), (1,)))
            row_term = jnp.sum(p * grad_p, axis=0, keepdims=True)
            grad_s = (p * (grad_p - row_term) * scale).astype(BF16)
            dq_t = dot(kg[t, :, cols], grad_s, ((0,), (0,)))
            dq[t, :, cols] = dq_t.T.astype(BF16)
            dk = dot(grad_s, q[t, :, cols], ((1,), (0,)))
            dv = dot(p.astype(BF16), grad_rows, ((1,), (0,)))
            dk_own[t, :, cols] = dk[:HALF]
            dv_own[t, :, cols] = dv[:HALF]
            dk_send[t, :, cols] = dk[HALF:].astype(BF16)
            dv_send[t, :, cols] = dv[HALF:].astype(BF16)
        for which, (src, dst) in enumerate(((dk_send, dk_recv), (dv_send, dv_recv))):
            n = (t * pairs + i) * 2 + which
            piece = pair_cols(near[i])
            copy = send(
                src.at[t, :, piece], dst.at[t, :, piece], grad_send_sem.at[n],
                grad_recv_sem.at[n], {"seq": partners[t]},
            )
            grads.append((copy, t))

    hd = heads * HDIM
    col_width = min(512, width)

    def weight_rows(i):
        r = far[i]
        if i == 0:
            for copy in load_go:
                copy.wait()
        left = attn_t[pair_cols(r), :]

        def tile(n, carry):
            cols = wide(n * col_width, col_width)
            right = go[:, :, cols].reshape(2 * HALF, col_width)
            block = dot(left, right, ((1,), (0,))).astype(BF16)
            wg[pl.ds(r * 8, 8), :, :, cols] = block.reshape(8, CORES, 16, col_width)
            return carry

        lax.fori_loop(0, width // col_width, tile, 0)
        rss.append(
            send(
                wg.at[pl.ds(r * 8, 8), 1 - c], sib_recv.at[pl.ds(r * 8, 8)], rss_send_sem.at[i],
                rss_recv_sem.at[i], {"seq": sibling},
            )
        )

    def grad_attn(i):
        for k in range(i + 2):
            for way in (1, -1):
                for key in ((way, k), (way, k, 1)):
                    if key in ag_sib and key not in ag_here:
                        ag_sib[key].wait_recv()
                        ag_here.append(key)
        if i == 0:
            ag_sib[0, 0].wait_recv()
        rows = w[pl.ds(near[i] * 8, 8)].reshape(HALF, width)
        tile = dot(go[...].reshape(2 * HALF, width), rows, ((1,), (1,)))
        ga[:, pair_cols(near[i])] = tile.astype(BF16)

    rss, ag_here = [], []

    rsw = {}

    def aside(way, k):
        i = len(rsw)
        first_row = (z + way * k + n_z) % n_z * n_y

        def add_cores(j, carry):
            for part in range(2):
                cols = wide(other + part * quarter, quarter)
                total = wg[first_row + j, c, :, cols].astype(F32)
                total = total + sib_recv[first_row + j, :, cols].astype(F32)
                side_send[i, part, j] = total.astype(BF16)
            return carry

        lax.fori_loop(0, n_y, add_cores, 0)
        rsw[way, k] = i, [
            send(
                side_send.at[i, part], side_recv.at[i, part], rsw_send_sem.at[2 * i + part],
                rsw_recv_sem.at[2 * i + part], {"dp": peer},
            )
            for part, peer in enumerate((x_next, x_prev))
        ]

    def aside_level(level):
        rss[level].wait_recv()
        k = n_plus - level
        aside(1, k)
        if k <= n_minus:
            aside(-1, k)
        if k == 1:
            aside(1, 0)

    rsp, rsm = {}, {}

    def chain(way, k):
        i, copies = rsw[way, k]
        first_row = (z + way * k + n_z) % n_z * n_y
        for copy in copies:
            copy.wait_recv()
        arrivals = []
        if (way == 1 or k == 0) and k < n_plus:
            rsp[k + 1].wait_recv()
            arrivals.append(plus_recv)
        if (way == -1 or k == 0) and k < n_minus:
            rsm[k + 1].wait_recv()
            arrivals.append(minus_recv)

        def add(j, carry):
            for part in range(2):
                cols = wide(mine + part * quarter, quarter)
                here = pl.ds(part * quarter, quarter)
                total = wg[first_row + j, c, :, cols].astype(F32)
                total = total + sib_recv[first_row + j, :, cols].astype(F32)
                total = total + side_recv[i, part, j].astype(F32)
                for ref in arrivals:
                    total = total + ref[k, j, :, here].astype(F32)
                if k == 0:
                    z_sum[j, :, here] = total
                    y_send[j, :, here] = total.astype(BF16)
                elif way == 1:
                    plus_send[k - 1, j, :, here] = total.astype(BF16)
                else:
                    minus_send[k - 1, j, :, here] = total.astype(BF16)
            return carry

        lax.fori_loop(0, n_y, add, 0)
        if k and way == 1:
            rsp[k] = send(
                plus_send.at[k - 1], plus_recv.at[k - 1], rsp_send_sem.at[k - 1],
                rsp_recv_sem.at[k - 1], {"seq": z_next},
            )
        if k and way == -1:
            rsm[k] = send(
                minus_send.at[k - 1], minus_recv.at[k - 1], rsm_send_sem.at[k - 1],
                rsm_recv_sem.at[k - 1], {"seq": z_prev},
            )

    def chain_level(k):
        if k <= n_plus:
            chain(1, k)
        if 0 < k <= n_minus:
            chain(-1, k)

    stores = []

    def store(src, dst):
        copy = pltpu.make_async_copy(src, dst, store_sem.at[len(stores)])
        copy.start()
        stores.append(copy)

    rsy, rsx = [], []

    def along_y(_):
        for j, peer in enumerate(y_peers, 1):
            rsy.append(
                send(
                    y_send.at[(y + j) % n_y], y_recv.at[j - 1], rsy_send_sem.at[j - 1],
                    rsy_recv_sem.at[j - 1], {"seq": peer},
                )
            )

    def along_x(_):
        total = z_sum[y]
        for j, copy in enumerate(rsy):
            copy.wait_recv()
            total = total + y_recv[j].astype(F32)
        x_all[x] = total.astype(BF16)
        for j, peer in enumerate(x_peers):
            rsx.append(
                send(
                    x_all.at[x], x_all.at[x], rsx_send_sem.at[j], rsx_recv_sem.at[j],
                    {"dp": peer},
                )
            )

    def last_sum(_):
        for copy in rsx:
            copy.wait_recv()
        for parity in range(2):
            total = x_all[parity].astype(F32)
            for j in range(parity + 2, n_x, 2):
                total = total + x_all[j].astype(F32)
            wgrad[:, pl.ds(parity * half, half)] = total * (1.0 / norm)
        store(wgrad, wgrad_hbm)

    def keep(_):
        for t in range(2):
            store(attn.at[pl.ds(t * HALF, HALF)], attn_hbm.at[token_rows(t)])
        store(w, w_hbm)

    def grad_sum(t):
        store(dq.at[t], dq_hbm.at[token_rows(t)])
        for copy, slot in grads:
            if slot == t:
                copy.wait()
        for own, got, out, hbm in (
            (dk_own, dk_recv, dk_send, dk_hbm), (dv_own, dv_recv, dv_send, dv_hbm)
        ):
            def add_rows(i, carry, own=own, got=got, out=out):
                rows = pl.ds(pl.multiple_of(i * 32, 32), 32)
                out[t, rows] = (own[t, rows] + got[t, rows].astype(F32)).astype(BF16)
                return carry

            lax.fori_loop(0, HALF // 32, add_rows, 0)
            store(out.at[t], hbm.at[token_rows(t)])

    plan = PLAN if n_z == 8 else SMALL_PLAN
    steps = {
        "hs": functools.partial(share_keys, 1),
        "ag": ag_step, "f0": functools.partial(forward, 0), "f1": functools.partial(forward, 1),
        "wg": weight_rows, "xs": aside_level, "zs": chain_level, "ga": grad_attn,
        "b0": functools.partial(backward, 0), "b1": functools.partial(backward, 1),
        "ys": along_y, "yx": along_x, "xx": last_sum, "kp": keep, "gs": grad_sum,
    }
    for item in " ".join(plan).split():
        steps[item[:2]](int(item[2:]))

    waited = [copy for copy, _ in grads]
    for copy in sent:
        if not any(copy is other for other in waited):
            copy.wait_send()
    for copy in stores:
        copy.wait()


def layer_kernel(
    attn_hbm, w_hbm, dq_in, dk_in, dv_in, wgrad_in,
    layer_hbm, dq_out, dk_out, dv_out, wgrad_out,
    attn, w, layer, dq, dk, dv, wgrad,
    load_sem, store_sem, in_sem, out_sem,
):
    hd, width = attn.shape[1], layer.shape[1]
    size = width // LAYER_PARTS
    parts = [pl.ds(n * size, size) for n in range(LAYER_PARTS)]
    loads = [pltpu.make_async_copy(attn_hbm, attn, load_sem.at[LAYER_PARTS])]
    for n, cols in enumerate(parts):
        loads.append(
            pltpu.make_async_copy(
                w_hbm.at[:, :, :, cols], w.at[:, :, :, cols], load_sem.at[n]
            )
        )
    moved = (
        (dq_in, dq, dq_out), (dk_in, dk, dk_out), (dv_in, dv, dv_out), (wgrad_in, wgrad, wgrad_out)
    )
    moves = [
        pltpu.make_async_copy(source, held, in_sem.at[n])
        for n, (source, held, _) in enumerate(moved)
    ]
    for copy in loads + moves:
        copy.start()
    stores = []
    loads[0].wait()
    for n, cols in enumerate(parts):
        loads[n + 1].wait()
        right = w[:, :, :, cols].reshape(hd, size)
        layer[:, cols] = dot(attn[...], right, ((1,), (0,))).astype(BF16)
        stores.append(
            pltpu.make_async_copy(layer.at[:, cols], layer_hbm.at[:, cols], store_sem.at[n])
        )
        stores[-1].start()
        if n < len(moved):
            _, held, target = moved[n]
            moves[n].wait()
            stores.append(pltpu.make_async_copy(held, target, out_sem.at[n]))
            stores[-1].start()
    for copy in stores:
        copy.wait()


def body(n_seq, n_x, n_y, queries, memory_keys, memory_values, out_weight, grad_out, key_first, key_last):
    rows, hd = queries.shape[1:]
    width = grad_out.shape[2]
    heads = hd // HDIM
    n_z = n_seq // (CORES * n_y)
    n_plus = n_z // 2
    n_minus = n_z - 1 - n_plus
    n_zy = n_z * n_y
    norm = math.sqrt(n_seq * rows)
    sizes = (n_seq, n_x, n_y, n_z, n_plus, n_minus, heads, width, norm)
    vmem, dma = pltpu.VMEM, pltpu.SemaphoreType.DMA
    scratch = [
        vmem((n_zy, CORES, 16, width), BF16),
        vmem((2, HALF, hd), BF16),
        vmem((2, 2 * HALF, hd), BF16),
        vmem((2, 2 * HALF, hd), BF16),
        vmem((2, HALF, width), BF16),
        vmem((2, heads, 2 * HALF, HALF), F32),
        vmem((hd, 2 * HALF), BF16),
        vmem((2 * HALF, hd), BF16),
        vmem((2 * HALF, hd), BF16),
        vmem((2, 2 * HALF, HALF), F32),
        vmem((2, HALF, hd), BF16),
        vmem((2, HALF, hd), F32),
        vmem((2, HALF, hd), F32),
        vmem((2, HALF, hd), BF16),
        vmem((2, HALF, hd), BF16),
        vmem((2, HALF, hd), BF16),
        vmem((2, HALF, hd), BF16),
        vmem((n_zy, CORES, 16, width), BF16),
        vmem((n_zy, 16, width), BF16),
        vmem((n_z, 2, n_y, 16, width // 4), BF16),
        vmem((n_z, 2, n_y, 16, width // 4), BF16),
        vmem((n_plus, n_y, 16, width // 2), BF16),
        vmem((n_plus, n_y, 16, width // 2), BF16),
        vmem((max(n_minus, 1), n_y, 16, width // 2), BF16),
        vmem((max(n_minus, 1), n_y, 16, width // 2), BF16),
        vmem((n_y, 16, width // 2), F32),
        vmem((n_y, 16, width // 2), BF16),
        vmem((n_y - 1, 16, width // 2), BF16),
        vmem((n_x, 16, width // 2), BF16),
        vmem((16, width), F32),
        dma((9,)),
        dma((10,)),
        dma((2 * n_z,)), dma((2 * n_z,)),
        dma((n_y - 1,)), dma((n_y - 1,)),
        dma((n_plus,)), dma((n_plus,)),
        dma((max(n_minus, 1),)), dma((max(n_minus, 1),)),
        dma((2 * n_z,)), dma((2 * n_z,)),
        dma((2 * n_z,)), dma((2 * n_z,)),
        dma((2 * n_z,)), dma((2 * n_z,)),
        dma((hd // HALF,)), dma((hd // HALF,)),
        dma((n_plus,)), dma((n_plus,)),
        dma((max(n_minus, 1),)), dma((max(n_minus, 1),)),
        dma((n_y - 1,)), dma((n_y - 1,)),
        dma((n_x - 1,)), dma((n_x - 1,)),
        dma((2 * n_z,)), dma((2 * n_z,)),
    ]
    hbm = pl.BlockSpec(memory_space=pl.ANY)
    smem = pl.BlockSpec(memory_space=pltpu.SMEM)
    attn, weight, *grads = pl.pallas_call(
        functools.partial(kernel, sizes),
        out_shape=(
            jax.ShapeDtypeStruct((rows, hd), BF16),
            jax.ShapeDtypeStruct((n_zy, CORES, 16, width), BF16),
            jax.ShapeDtypeStruct((rows, hd), BF16),
            jax.ShapeDtypeStruct((rows, hd), BF16),
            jax.ShapeDtypeStruct((rows, hd), BF16),
            jax.ShapeDtypeStruct((16, width), F32),
        ),
        in_specs=[hbm] * 5 + [smem] * 2,
        out_specs=(hbm,) * 6,
        scratch_shapes=scratch,
        compiler_params=pltpu.CompilerParams(
            collective_id=0, has_side_effects=True, vmem_limit_bytes=60 * 1024 * 1024
        ),
    )(
        queries[0], memory_keys[0], memory_values[0], out_weight, grad_out[0], key_first, key_last
    )
    layer_out, *grads = pl.pallas_call(
        layer_kernel,
        out_shape=(
            jax.ShapeDtypeStruct((rows, width), BF16),
            *(jax.ShapeDtypeStruct(grad.shape, grad.dtype) for grad in grads),
        ),
        in_specs=[hbm] * 6,
        out_specs=(hbm,) * 5,
        scratch_shapes=[
            vmem((rows, hd), BF16),
            vmem((n_zy, CORES, 16, width), BF16),
            vmem((rows, width), BF16),
            *(vmem(grad.shape, grad.dtype) for grad in grads),
            dma((LAYER_PARTS + 1,)), dma((LAYER_PARTS,)), dma((4,)), dma((4,)),
        ],
        compiler_params=pltpu.CompilerParams(vmem_limit_bytes=60 * 1024 * 1024),
    )(attn, weight, *grads)
    weight_grad = grads.pop()
    return (layer_out[None], *(grad[None] for grad in grads), weight_grad)


def solution(mesh, n_y=Y_CHIPS):
    return jax.shard_map(
        functools.partial(body, mesh.shape["seq"], mesh.shape["dp"], n_y),
        mesh=mesh,
        in_specs=(
            P("dp", "seq", None),
            P("dp", "seq", None),
            P("dp", "seq", None),
            P("seq", None),
            P("dp", "seq", None),
            P("dp", "seq"),
            P("dp", "seq"),
        ),
        out_specs=(
            P("dp", "seq", None),
            P("dp", "seq", None),
            P("dp", "seq", None),
            P("dp", "seq", None),
            P("seq", None),
        ),
        check_vma=False,
    )
```
